512 devices in a mesh: dp: 64 (over y, z), mp: 8 (over x, core).
Axes of the slice: x: 4, y: 4, z: 16, core: 2. Of those that a mesh axis runs over, the one named last changes fastest.
Arguments:
- tokens: bfloat16 [32768, 8192], P('dp', 'mp'), may hold values from -6 to 6
- base_weight: bfloat16 [8192, 1024], P('mp'), may hold values from -0.0625 to 0.0625
- adapter_a: bfloat16 [128, 8192, 64], P('dp', 'mp'), may hold values from -0.0625 to 0.0625
- adapter_b: bfloat16 [128, 64, 1024], P('dp', None, 'mp'), may hold values from -0.75 to 0.75
- row_ids: int32 [32768], P('dp'), may hold values from 0 to 127, as said below
- panel_of: int32 [128], replicated, may hold values from 0 to 127, as said below
- stop_flags: int32 [128], P('dp'), may hold values 0 or 1
- upstream: bfloat16 [32768, 1024], P('dp', 'mp'), may hold values from -6 to 6
Outputs:
- projected: bfloat16 [32768, 1024], P('dp', 'mp')
- token_input_gradient: bfloat16 [32768, 8192], P('dp', 'mp')
- down_gradient: bfloat16 [128, 8192, 64], P('dp', 'mp')
- up_gradient: bfloat16 [128, 64, 1024], P('dp', None, 'mp')
The draws below stay inside these ranges and needn't reach their ends.
Inputs may be any that keep to these rules, and one draw needn't show every extreme that they name: `row_ids`: within the rows of one index of dp the ids never fall; those rows name exactly 64 adapters, one of the panels of every owner (owner = panel_of[id] // 2); at most 10 rows of one index of dp belong to the panels of one owner, and every index of dp has some owner with exactly 10 of its rows. `panel_of`: each panel number appears once; panel p is owned by index p // 2 of dp.
All inputs are finite; a program needn't handle non-finite values. No bound on the sum of `stop_flags` on one device may be relied on, other than what follows from the above.
Results may differ from the reference program's by a relative error of at most 0.0055.
Values may be sent and summed in bfloat16 or wider, within the bound.
A program may use at most 64 MiB of HBM per device.

```python
import jax
import jax.numpy as jnp
from jax import lax

D = 8192
KV = 1024
R = 64
ADP_DEV = 2
TOK_DEV = 512
ADAPTER_COUNT = 128
SEGS = 64
CAPD = 10
TOKENS = 32768
N_DP = 64


def panel_order(key):
    return jax.random.permutation(jax.random.fold_in(key, 11), ADAPTER_COUNT).astype(jnp.int32)


def draw_panel_of(key, part):
    return jnp.argsort(panel_order(key)).astype(jnp.int32)


def draw_row_ids(key, part):
    order = panel_order(key)
    devices = TOKENS // TOK_DEV
    mean_len = TOK_DEV // SEGS
    quarter = mean_len // 4

    def one_device(dkey):
        keys = jax.random.split(dkey, 4)
        shifts = jax.random.randint(keys[0], (SEGS // 2,), -quarter, quarter + 1)
        shifts = shifts.at[0].set(quarter)
        lengths = jnp.concatenate([mean_len + shifts, mean_len - shifts])
        lengths = lengths[jax.random.permutation(keys[1], SEGS)]
        picked = jnp.arange(devices, dtype=jnp.int32)
        within = jax.random.randint(keys[3], (SEGS,), 0, ADP_DEV)
        names = jnp.sort(order[picked * ADP_DEV + within])
        names = names[jax.random.permutation(keys[2], SEGS)]
        names = jnp.sort(names)
        ends = jnp.cumsum(lengths)
        positions = jnp.arange(TOK_DEV, dtype=jnp.int32)
        segment = jnp.sum((positions[:, None] >= ends[None, :]).astype(jnp.int32), axis=1)
        return names[segment]
    all_keys = jax.random.split(jax.random.fold_in(key, 3), devices)
    return jax.vmap(one_device)(all_keys).reshape(TOKENS).astype(jnp.int32)


def place_ends(drawn, own_key, least, top_value):
    spot = [jax.random.randint(jax.random.fold_in(own_key, axis), (), 0, length) for axis, length in enumerate(drawn.shape)]
    main_axis = drawn.shape.index(max(drawn.shape))
    neighbour = spot[:main_axis] + [(spot[main_axis] + 1) % drawn.shape[main_axis]] + spot[main_axis + 1:]
    return drawn.at[tuple(spot)].set(least).at[tuple(neighbour)].set(top_value)


def levels(own_key, extent, cuts, smallest, high):
    gain, own = 1.0, jax.random.fold_in(own_key, 6)
    for axis_at, shards_of in cuts:
        steps = jnp.exp(jax.random.uniform(jax.random.fold_in(own, axis_at), (shards_of,), jnp.float32, smallest / len(cuts), high / len(cuts)))
        gain = gain * jnp.repeat(steps, extent[axis_at] // shards_of).reshape([-1 if axis == axis_at else 1 for axis in range(len(extent))])
    return gain


def normal_values(stream_key, dims, scale, reach, pieces=(), held_as=jnp.bfloat16):
    loudness = levels(stream_key, dims, pieces, -0.22, 0.18) if pieces else 1.0
    drawn = jax.random.normal(stream_key, dims, jnp.float32) * scale * loudness
    return jnp.minimum(jnp.maximum(drawn, -reach), reach).astype(held_as)


def setup_inputs(seed: int = 0) -> dict:
    splits = jax.random.split(jax.random.key(seed), 9)
    tokens = normal_values(splits[0], (TOKENS, D), 1.0, 6.0, ((0, 64), (1, 8)))
    base_weight = normal_values(splits[1], (D, KV), D ** -0.5, 0.0625, ((0, 8),))
    adapter_a = normal_values(splits[2], (ADAPTER_COUNT, D, R), D ** -0.5, 0.0625, ((0, 64), (1, 8)))
    adapter_b = normal_values(splits[3], (ADAPTER_COUNT, R, KV), R ** -0.5, 0.75, ((0, 64), (2, 8)))
    row_ids = draw_row_ids(jax.random.fold_in(splits[8], 71), 0)
    panel_of = draw_panel_of(jax.random.fold_in(splits[8], 71), 0)
    stop_flags = place_ends((jax.random.randint(splits[6], (ADAPTER_COUNT,), 0, 3) < 1).astype(jnp.int32), jax.random.fold_in(splits[6], 1), 0, 1)
    upstream = normal_values(splits[7], (TOKENS, KV), 1.0, 6.0, ((0, 64), (1, 8)))
    return {"tokens": tokens, "base_weight": base_weight, "adapter_a": adapter_a, "adapter_b": adapter_b, "row_ids": row_ids, "panel_of": panel_of, "stop_flags": stop_flags, "upstream": upstream}


adapter_scale = 2.0


def reference(tokens, base_weight, adapter_a, adapter_b, row_ids, panel_of, stop_flags, upstream):
    frozen_matrix = jnp.dot(tokens, base_weight, preferred_element_type=jnp.float32)
    frozen_gradient = jnp.dot(upstream, base_weight.T, preferred_element_type=jnp.float32)
    panel = panel_of[row_ids].astype(jnp.int32)
    order = jnp.argsort(panel, stable=True).astype(jnp.int32)
    counts = jnp.sum((panel[None, :] == jnp.arange(ADAPTER_COUNT, dtype=jnp.int32)[:, None]).astype(jnp.int32), axis=1)
    starts = jnp.cumsum(counts) - counts
    spread = N_DP * CAPD
    offsets = jnp.arange(spread, dtype=jnp.int32)

    def single_panel(loop_carry, number):
        adapter_accumulator, gradient_accumulator = loop_carry
        valid_mask = offsets < counts[number]
        selected_adapter = order[jnp.minimum(starts[number] + offsets, TOKENS - 1)]
        incoming_rows = jnp.where(valid_mask[:, None], tokens[selected_adapter], 0)
        incoming_gradients = jnp.where(valid_mask[:, None], upstream[selected_adapter], 0)
        down_panel = adapter_a[number]
        up_panel = adapter_b[number]
        rank_activation = jnp.dot(incoming_rows, down_panel, preferred_element_type=jnp.float32).astype(jnp.bfloat16)
        backward_result = jnp.dot(incoming_gradients, up_panel.T, preferred_element_type=jnp.float32).astype(jnp.bfloat16)
        adapter_delta = (adapter_scale * jnp.dot(rank_activation, up_panel, preferred_element_type=jnp.float32)).astype(jnp.bfloat16)
        adapter_gradient = (adapter_scale * jnp.dot(backward_result, down_panel.T, preferred_element_type=jnp.float32)).astype(jnp.bfloat16)
        active_mask = (1 - stop_flags[number]).astype(jnp.float32)
        panel_down_gradient = (adapter_scale * active_mask * jnp.dot(incoming_rows.T, backward_result, preferred_element_type=jnp.float32)).astype(jnp.bfloat16)
        panel_up_gradient = (adapter_scale * active_mask * jnp.dot(rank_activation.T, incoming_gradients, preferred_element_type=jnp.float32)).astype(jnp.bfloat16)
        adapter_accumulator = adapter_accumulator.at[selected_adapter].add(jnp.where(valid_mask[:, None], adapter_delta, 0))
        gradient_accumulator = gradient_accumulator.at[selected_adapter].add(jnp.where(valid_mask[:, None], adapter_gradient, 0))
        return (adapter_accumulator, gradient_accumulator), (panel_down_gradient, panel_up_gradient)

    initial_carry = (jnp.zeros((TOKENS, KV), jnp.bfloat16), jnp.zeros((TOKENS, D), jnp.bfloat16))
    (adapter_delta_total, adapter_gradient_total), (down_gradient, up_gradient) = lax.scan(single_panel, initial_carry, jnp.arange(ADAPTER_COUNT, dtype=jnp.int32))
    projected = (frozen_matrix + adapter_delta_total.astype(jnp.float32)).astype(jnp.bfloat16)
    token_input_gradient = (frozen_gradient + adapter_gradient_total.astype(jnp.float32)).astype(jnp.bfloat16)
    return (projected, token_input_gradient, down_gradient, up_gradient)
```

```python
import jax
import jax.numpy as jnp
from jax import lax
from jax.experimental import pallas as pl
from jax.experimental.pallas import tpu as pltpu
from jax.sharding import Mesh
from jax.sharding import PartitionSpec as P

SCALE = 2.0
F32 = jnp.float32
BF16 = jnp.bfloat16
NY, NZ, NX, NC = 4, 16, 4, 2
NM = NX * NC
PAD = 16
FAR = NZ // 2
DP = ("y", "z")
MP = ("x", "core")
BATCHES = ((0, 9), (9, 13), (13, 16))
CHUNKS = 2 * FAR - 1


def dot(a, b, ca, cb):
    return lax.dot_general(a, b, (((ca,), (cb,)), ((), ())), preferred_element_type=F32)


def below(s):
    return 0 if s == 0 else (NZ - 1 if s == FAR else 2 * s - 1)


def above(s):
    return 0 if s == 0 else (NZ - 1 if s == FAR else 2 * s)


def kernel(packed, send, ret, total, panels, rbuf, rets, pk, rsr, pkf, part, psend, prec,
           ag_s, ag_r, y_s, y_r, rt_s, rt_r, xs_s, xs_r, xg_s, xg_r, rs_s, rs_r, loc):
    feats = packed.shape[1] - 128
    half = packed.shape[0] // 2
    yi, zi, xi, ci = (lax.axis_index(n) for n in ("y", "z", "x", "core"))
    m = xi * NC + ci
    up = {"z": lax.rem(zi + 1, NZ)}
    down = {"z": lax.rem(zi + NZ - 1, NZ)}

    def y_peer(d):
        return {"y": lax.rem(yi + d, NY)}

    def m_peer(d):
        p = lax.rem(m + d, NM)
        return {"x": p // NC, "core": lax.rem(p, NC)}

    bar = pltpu.get_barrier_semaphore()
    peers = [up, down] + [y_peer(d) for d in range(1, NY)] + [m_peer(d) for d in range(1, NM)]
    for p in peers:
        pl.semaphore_signal(bar, inc=1, device_id=p, device_id_type=pl.DeviceIdType.MESH)
    pl.semaphore_wait(bar, len(peers))

    started = []

    def remote(src, dst, ssem, rsem, dev):
        c = pltpu.make_async_remote_copy(
            src_ref=src, dst_ref=dst, send_sem=ssem, recv_sem=rsem, device_id=dev,
            device_id_type=pl.DeviceIdType.MESH,
        )
        return c

    def go(*a):
        c = remote(*a)
        c.start()
        started.append(c)

    def ag_start(c):
        s, h = c // 2, c % 2
        for w, (dev, here, there) in enumerate(
            ((up, below(s), below(s + 1)), (down, above(s), above(s + 1)))
        ):
            hh = h if w == 0 else 1 - h
            rows = pl.ds(half * hh, half)
            src = packed.at[rows] if s == 0 else panels.at[here, rows]
            go(src, panels.at[there, rows], ag_s.at[w, c], ag_r.at[w, c], dev)

    def ag_wait(c):
        s, h = c // 2, c % 2
        for w, (dev, there) in enumerate(((up, below(s + 1)), (down, above(s + 1)))):
            hh = h if w == 0 else 1 - h
            ref = panels.at[there, pl.ds(half * hh, half)]
            remote(ref, ref, ag_s.at[w, c], ag_r.at[w, c], dev).wait_recv()

    ag_start(0)
    ag_start(1)
    mine_rows = pl.ds(pl.multiple_of(yi * PAD, PAD), PAD)
    for d in range(1, NY):
        go(send.at[lax.rem(yi + d, NY)], rbuf.at[:, mine_rows, :], y_s.at[d], y_r.at[d], y_peer(d))
    own = pltpu.make_async_copy(send.at[yi], rbuf.at[:, mine_rows, :], loc.at[0])
    own.start()
    panels[0] = packed[...]

    lane = lax.broadcasted_iota(jnp.int32, (NY * PAD, 128), 1) < 64

    def masks(k):
        v = rbuf[k, :, feats:].astype(F32).reshape(NY, PAD, 128)[:, PAD - 1 :, :]
        return jnp.broadcast_to(v, (NY, PAD, 128)).reshape(NY * PAD, 128)

    def rows_wait():
        own.wait()
        for d in range(1, NY):
            src = rbuf.at[:, pl.ds(pl.multiple_of(lax.rem(yi + NY - d, NY) * PAD, PAD), PAD), :]
            remote(src, src, y_s.at[d], y_r.at[d], y_peer(d)).wait_recv()

    def first(k):
        mask = masks(k)
        inner = dot(rbuf[k, :, :feats], panels[k, :, :feats], 1, 1) * mask
        back = dot(rbuf[k, :, feats:], panels[k, :, feats:], 1, 1) * mask
        inner = inner + pltpu.roll(inner, 64, 1)
        back = back + pltpu.roll(back, 64, 1)
        pk[k] = jnp.where(lane, inner, back)

    def x_send(b):
        k0, k1 = BATCHES[b]
        for d in range(1, NM):
            p = lax.rem(m + d, NM)
            go(pk.at[k0:k1, pl.ds(pl.multiple_of(p * 8, 8), 8), :], rsr.at[m, k0:k1],
               xs_s.at[b, d], xs_r.at[b, d], m_peer(d))

    def x_reduce(b):
        k0, k1 = BATCHES[b]
        mine = pl.ds(pl.multiple_of(m * 8, 8), 8)
        acc = pk[k0:k1, mine, :]
        for d in range(1, NM):
            src = lax.rem(m + NM - d, NM)
            ref = rsr.at[src, k0:k1]
            remote(ref, ref, xs_s.at[b, d], xs_r.at[b, d], m_peer(d)).wait_recv()
            acc = acc + rsr[src, k0:k1]
        pkf[k0:k1, mine, :] = acc.astype(BF16).astype(F32)
        for d in range(1, NM):
            ref = pkf.at[k0:k1, mine, :]
            go(ref, ref, xg_s.at[b, d], xg_r.at[b, d], m_peer(d))

    def x_finish(b):
        k0, k1 = BATCHES[b]
        for d in range(1, NM):
            src = lax.rem(m + NM - d, NM)
            ref = pkf.at[k0:k1, pl.ds(pl.multiple_of(src * 8, 8), 8), :]
            remote(ref, ref, xg_s.at[b, d], xg_r.at[b, d], m_peer(d)).wait_recv()

    def spread(k):
        mask = masks(k)
        v = pkf[k]
        r = pltpu.roll(v, 64, 1)
        return (jnp.where(lane, v, r) * mask).astype(BF16), (jnp.where(lane, r, v) * mask).astype(BF16)

    def sums(k):
        inner, back = spread(k)
        part[k, :, :feats] = dot(back, rbuf[k, :, :feats], 0, 0)
        part[k, :, feats:] = dot(inner, rbuf[k, :, feats:], 0, 0)

    def rows_back(k):
        inner, back = spread(k)
        grad = (SCALE * dot(back, panels[k, :, :feats], 1, 0)).astype(BF16)
        delta = (SCALE * dot(inner, panels[k, :, feats:], 1, 0)).astype(BF16)
        for q in range(NY):
            rets[q, k, :, :feats] = grad[q * PAD : (q + 1) * PAD]
            rets[q, k, :, feats:] = delta[q * PAD : (q + 1) * PAD]

    locals_ = [own]

    def ret_send(i, k0, k1):
        for d in range(1, NY):
            go(rets.at[lax.rem(yi + d, NY), k0:k1], ret.at[yi, k0:k1], rt_s.at[i, d], rt_r.at[i, d], y_peer(d))
        c = pltpu.make_async_copy(rets.at[yi, k0:k1], ret.at[yi, k0:k1], loc.at[1 + i])
        c.start()
        locals_.append(c)

    def ret_wait(i, k0, k1):
        locals_[1 + i].wait()
        for d in range(1, NY):
            ref = ret.at[lax.rem(yi + NY - d, NY), k0:k1]
            remote(ref, ref, rt_s.at[i, d], rt_r.at[i, d], y_peer(d)).wait_recv()

    def ag_step(c):
        ag_wait(c)
        if c + 2 < CHUNKS:
            ag_start(c + 2)

    for c in range(9):
        ag_step(c)
    rows_wait()
    for k in range(3):
        first(k)
    ag_step(9)
    for k in range(3, 6):
        first(k)
    ag_step(10)
    for k in range(6, 9):
        first(k)
    x_send(0)
    ag_step(11)
    first(9)
    first(10)
    x_reduce(0)
    ag_step(12)
    first(11)
    first(12)
    x_send(1)
    x_finish(0)
    rows_back(0)
    ag_step(13)
    first(13)
    first(14)
    x_reduce(1)
    ag_step(14)
    first(15)
    x_send(2)
    x_finish(1)
    for k in range(1, 5):
        rows_back(k)
    x_reduce(2)
    for k in range(5, 8):
        rows_back(k)
    ret_send(0, 0, 8)
    x_finish(2)

    def piece(w, c):
        s, h = FAR - (c + 1) // 2, (c % 2 if c else 0)
        hh = h if w == 0 else 1 - h
        return (above(s) if w == 0 else below(s)), pl.ds(half * hh, half)

    def rs_step(c):
        for w, dev in enumerate((up, down)):
            k, rows = piece(w, c)
            v = part[k, rows, :]
            if c >= 2:
                ref = prec.at[w, c - 2]
                remote(ref, ref, rs_s.at[w, c - 2], rs_r.at[w, c - 2], dev).wait_recv()
                v = v + prec[w, c - 2].astype(F32)
            psend[w, c] = v.astype(BF16)
            go(psend.at[w, c], prec.at[w, c], rs_s.at[w, c], rs_r.at[w, c], dev)

    sums(15)
    rs_step(0)
    sums(14)
    sums(13)
    rs_step(1)
    rows_back(8)
    rows_back(9)
    rs_step(2)
    for i, s in enumerate(range(6, 0, -1)):
        sums(2 * s)
        sums(2 * s - 1)
        rs_step(3 + 2 * i)
        if i < 3:
            rows_back(10 + 2 * i)
            rows_back(11 + 2 * i)
        if i == 2:
            ret_send(1, 8, 16)
        rs_step(4 + 2 * i)
    sums(0)
    ret_wait(0, 0, 8)
    ret_wait(1, 8, 16)
    for w, dev in enumerate((up, down)):
        for c in (CHUNKS - 2, CHUNKS - 1):
            ref = prec.at[w, c]
            remote(ref, ref, rs_s.at[w, c], rs_r.at[w, c], dev).wait_recv()
    first_half = part[0, :half] + prec[0, CHUNKS - 1].astype(F32) + prec[1, CHUNKS - 2].astype(F32)
    second_half = part[0, half:] + prec[0, CHUNKS - 2].astype(F32) + prec[1, CHUNKS - 1].astype(F32)
    total[:half] = first_half
    total[half:] = second_half
    for c in started:
        c.wait_send()


def exchange(packed, send):
    n, wide = packed.shape
    half = n // 2
    vm = pl.BlockSpec(memory_space=pltpu.VMEM)
    dma = pltpu.SemaphoreType.DMA
    rows = NY * PAD
    return pl.pallas_call(
        kernel,
        out_shape=(
            jax.ShapeDtypeStruct((NY, NZ, PAD, wide), BF16),
            jax.ShapeDtypeStruct((n, wide), F32),
        ),
        in_specs=[vm, vm],
        out_specs=(vm, vm),
        scratch_shapes=[
            pltpu.VMEM((NZ, n, wide), BF16),
            pltpu.VMEM((NZ, rows, wide), BF16),
            pltpu.VMEM((NY, NZ, PAD, wide), BF16),
            pltpu.VMEM((NZ, rows, 128), F32),
            pltpu.VMEM((NM, NZ, rows // NM, 128), F32),
            pltpu.VMEM((NZ, rows, 128), F32),
            pltpu.VMEM((NZ, n, wide), F32),
            pltpu.VMEM((2, CHUNKS, half, wide), BF16),
            pltpu.VMEM((2, CHUNKS, half, wide), BF16),
            dma((2, CHUNKS)), dma((2, CHUNKS)),
            dma((NY,)), dma((NY,)),
            dma((2, NY)), dma((2, NY)),
            dma((len(BATCHES), NM)), dma((len(BATCHES), NM)),
            dma((len(BATCHES), NM)), dma((len(BATCHES), NM)),
            dma((2, CHUNKS)), dma((2, CHUNKS)),
            dma((3,)),
        ],
        compiler_params=pltpu.CompilerParams(
            collective_id=0, has_side_effects=True, vmem_limit_bytes=56 * 2**20
        ),
        cost_estimate=pl.CostEstimate(flops=2 * 10**9, bytes_accessed=10**8, transcendentals=0),
    )(packed, send)


def shards(tokens, base_weight, adapter_a, adapter_b, row_ids, panel_of, stop_flags, upstream):
    rows = tokens.shape[0]
    per_owner, feats, rank = adapter_a.shape
    vals = upstream.shape[1]
    n_panels = panel_of.shape[0]
    owners = NY * NZ
    wide = feats + vals
    zi = lax.axis_index("z")
    packed = jnp.concatenate(
        [
            jnp.transpose(adapter_a, (0, 2, 1)).reshape(per_owner * rank, feats),
            adapter_b.reshape(per_owner * rank, vals),
        ],
        axis=1,
    )
    matches = row_ids[:, None] == jnp.arange(n_panels, dtype=jnp.int32)[None, :]
    panel = jnp.sum(jnp.where(matches, panel_of[None, :], 0), axis=1)
    owner = panel // per_owner
    within = panel % per_owner
    t = jnp.arange(rows, dtype=jnp.int32)
    earlier = jnp.sum(
        ((owner[:, None] == owner[None, :]) & (t[:, None] < t[None, :])).astype(jnp.int32), axis=0
    )
    away = (owner % NZ - zi + NZ) % NZ
    order = jnp.where(away == FAR, NZ - 1, jnp.where(away < FAR, 2 * away, 2 * (NZ - away) - 1))
    block = (owner // NZ) * NZ + order
    slot = block * PAD + earlier
    slots = owners * PAD
    place = (slot[None, :] == jnp.arange(slots, dtype=jnp.int32)[:, None]).astype(BF16)
    held = block[None, :] == jnp.arange(owners, dtype=jnp.int32)[:, None]
    which = jnp.max(jnp.where(held, within[None, :], 0), axis=1)
    both = jnp.concatenate([tokens, upstream], axis=1)
    col = jnp.arange(wide, dtype=jnp.int32)
    pick = ((col[None, :] - feats) // rank == which[:, None]) & (col[None, :] >= feats)
    last = jnp.arange(PAD, dtype=jnp.int32) == PAD - 1
    send = dot(place, both, 1, 0).reshape(owners, PAD, wide)
    send = jnp.where(last[None, :, None], pick.astype(F32)[:, None, :], send).astype(BF16)
    send = send.reshape(NY, NZ, PAD, wide)
    frozen_output = lax.psum_scatter(
        dot(base_weight, tokens, 0, 1), MP, scatter_dimension=0, tiled=True
    ).T
    all_up = lax.all_gather(upstream, MP, axis=1, tiled=True)
    frozen_gradient = dot(all_up, base_weight, 1, 1)
    ret, total = exchange(packed, send)
    mine = dot(place, ret.reshape(slots, wide), 0, 0)
    projected = (frozen_output + mine[:, feats:]).astype(BF16)
    token_input_gradient = (frozen_gradient + mine[:, :feats]).astype(BF16)
    active = (1 - stop_flags).astype(F32)
    scale = (SCALE * active)[:, None, None]
    down_gradient = scale * total[:, :feats].reshape(per_owner, rank, feats)
    up_gradient = scale * total[:, feats:].reshape(per_owner, rank, vals)
    return (
        projected,
        token_input_gradient,
        jnp.transpose(down_gradient, (0, 2, 1)).astype(BF16),
        up_gradient.astype(BF16),
    )


def solution(mesh):
    fine = Mesh(mesh.devices.reshape(NY, NZ, NX, NC), ("y", "z", "x", "core"))
    placed = (
        P(DP, MP),
        P(MP, None),
        P(DP, MP, None),
        P(DP, None, MP),
        P(DP),
        P(),
        P(DP),
        P(DP, MP),
    )
    return jax.shard_map(
        shards,
        mesh=fine,
        in_specs=placed,
        out_specs=(P(DP, MP), P(DP, MP), P(DP, MP, None), P(DP, None, MP)),
        check_vma=False,
    )
```

```python
import jax
import jax.numpy as jnp
from jax import lax
from jax.experimental import pallas as pl
from jax.experimental.pallas import tpu as pltpu
from jax.sharding import Mesh
from jax.sharding import PartitionSpec as P

SCALE = 2.0
F32 = jnp.float32
BF16 = jnp.bfloat16
NY, NZ, NX, NC = 4, 16, 4, 2
NM = NX * NC
PAD = 16
FAR = NZ // 2
DP = ("y", "z")
MP = ("x", "core")
BATCHES = ((0, 9), (9, 13), (13, 16))
CHUNKS = 2 * FAR - 1


def dot(a, b, ca, cb):
    return lax.dot_general(a, b, (((ca,), (cb,)), ((), ())), preferred_element_type=F32)


def below(s):
    return 0 if s == 0 else (NZ - 1 if s == FAR else 2 * s - 1)


def above(s):
    return 0 if s == 0 else (NZ - 1 if s == FAR else 2 * s)


def kernel(tok_hbm, w_hbm, at_ref, b_ref, ids_ref, panel_ref, flags_ref, up_ref,
           proj_ref, tig_ref, down_ref, upg_ref,
           tok, w, ua, fs, fr, fg, back_place, send, ret, panels, rbuf, rets, pk, rsr, pkf, part, psend, prec,
           ag_s, ag_r, y_s, y_r, rt_s, rt_r, xs_s, xs_r, xg_s, xg_r, rs_s, rs_r, u_s, u_r, f_s, f_r, loc):
    scope = jax.named_scope
    rows, feats = tok.shape
    wide = feats + 128
    half = at_ref.shape[0] // 2
    yi, zi, xi, ci = (lax.axis_index(n) for n in ("y", "z", "x", "core"))
    m = xi * NC + ci
    up = {"z": lax.rem(zi + 1, NZ)}
    down = {"z": lax.rem(zi + NZ - 1, NZ)}

    def y_peer(d):
        return {"y": lax.rem(yi + d, NY)}

    def m_peer(d):
        p = lax.rem(m + d, NM)
        return {"x": p // NC, "core": lax.rem(p, NC)}

    def lanes(p):
        return pl.ds(pl.multiple_of(p * 128, 128), 128)

    tok_in = pltpu.make_async_copy(tok_hbm, tok, loc.at[3])
    tok_in.start()
    w_in = pltpu.make_async_copy(w_hbm, w, loc.at[4])
    w_in.start()
    with scope("entry"):
        bar = pltpu.get_barrier_semaphore()
        peers = [up, down] + [y_peer(d) for d in range(1, NY)] + [m_peer(d) for d in range(1, NM)]
        for p in peers:
            pl.semaphore_signal(bar, inc=1, device_id=p, device_id_type=pl.DeviceIdType.MESH)
        panels[0, :, :feats] = at_ref[...]
        panels[0, :, feats:] = b_ref[...]
        pl.semaphore_wait(bar, len(peers))

    started = []

    def remote(src, dst, ssem, rsem, dev):
        return pltpu.make_async_remote_copy(
            src_ref=src, dst_ref=dst, send_sem=ssem, recv_sem=rsem, device_id=dev,
            device_id_type=pl.DeviceIdType.MESH,
        )

    def go(*a):
        c = remote(*a)
        c.start()
        started.append(c)

    def ag_start(c):
        s, h = c // 2, c % 2
        for v, (dev, here, there) in enumerate(
            ((up, below(s), below(s + 1)), (down, above(s), above(s + 1)))
        ):
            part_rows = pl.ds(half * (h if v == 0 else 1 - h), half)
            go(panels.at[here, part_rows], panels.at[there, part_rows], ag_s.at[v, c], ag_r.at[v, c], dev)

    def ag_step(c):
        s, h = c // 2, c % 2
        with scope(f"panel_hop_{c}"):
            for v, (dev, there) in enumerate(((up, below(s + 1)), (down, above(s + 1)))):
                ref = panels.at[there, pl.ds(half * (h if v == 0 else 1 - h), half)]
                remote(ref, ref, ag_s.at[v, c], ag_r.at[v, c], dev).wait_recv()
            if c + 2 < CHUNKS:
                ag_start(c + 2)

    ag_start(0)
    ag_start(1)

    def iota(shape, d):
        return lax.broadcasted_iota(jnp.int32, shape, d)

    def hot(cond):
        return jnp.where(cond, 1.0, 0.0)

    with scope("routing"):
        n_panels = panel_ref.shape[1]
        owners = NY * NZ
        rank = 64
        named = hot(iota((n_panels, rows), 0) == ids_ref[...]).astype(BF16)
        mapped = hot(iota((n_panels, n_panels), 0) == panel_ref[...]).astype(BF16)
        panel_hot = dot(mapped, named, 1, 0)
        panel = jnp.sum(panel_hot * iota((n_panels, rows), 0).astype(F32), axis=0, keepdims=True).astype(jnp.int32)
        owner = panel // 2
        within = panel - owner * 2
        own_y = owner // NZ
        away = owner - own_y * NZ - zi
        away = jnp.where(away < 0, away + NZ, away)
        order = jnp.where(away == FAR, NZ - 1, jnp.where(away < FAR, 2 * away, 2 * (NZ - away) - 1))
        block = own_y * NZ + order
        block_hot = hot(iota((owners, rows), 0) == block)
        before = hot(iota((rows, rows), 0) < iota((rows, rows), 1)).astype(BF16)
        counts = dot(block_hot.astype(BF16), before, 1, 0) * block_hot
        earlier = jnp.sum(counts, axis=0, keepdims=True).astype(jnp.int32)
        slot = block * PAD + earlier
        which = jnp.max(block_hot * within.astype(F32), axis=1, keepdims=True)
        pick = hot((iota((owners, 128), 1) // rank).astype(F32) == which)
        last = iota((NZ * PAD, 128), 0) % PAD == PAD - 1
        tok_in.wait()
    with scope("rows_out"):
        for q in range(NY):
            place = hot(iota((NZ * PAD, rows), 0) + q * NZ * PAD == slot).astype(BF16)
            t = dot(place, tok[...], 1, 0).astype(BF16)
            u = dot(place, up_ref[...], 1, 0)
            marks = jnp.broadcast_to(pick[q * NZ : (q + 1) * NZ].reshape(NZ, 1, 128), (NZ, PAD, 128))
            u = jnp.where(last, marks.reshape(NZ * PAD, 128), u).astype(BF16)
            send[q, :, :, :feats] = t.reshape(NZ, PAD, feats)
            send[q, :, :, feats:] = u.reshape(NZ, PAD, 128)
        mine_rows = pl.ds(pl.multiple_of(yi * PAD, PAD), PAD)
        for d in range(1, NY):
            go(send.at[lax.rem(yi + d, NY)], rbuf.at[:, mine_rows, :], y_s.at[d], y_r.at[d], y_peer(d))
        own = pltpu.make_async_copy(send.at[yi], rbuf.at[:, mine_rows, :], loc.at[0])
        own.start()
    ag_step(0)
    with scope("cotangents_out"):
        for d in range(1, NM):
            go(up_ref, ua.at[:, lanes(m)], u_s.at[d], u_r.at[d], m_peer(d))
        ua[:, lanes(m)] = up_ref[...]
        w_in.wait()
    with scope("base"):
        for j in range(NM // 2):
            r = dot(tok[...], w[:, 256 * j : 256 * j + 256], 1, 0)
            fs[2 * j] = r[:, :128]
            fs[2 * j + 1] = r[:, 128:]
    ag_step(1)
    with scope("base_out"):
        for d in range(1, NM):
            p = lax.rem(m + d, NM)
            go(fs.at[p], fr.at[m], f_s.at[d], f_r.at[d], m_peer(d))
    ag_step(2)
    with scope("row_places"):
        ones = jnp.ones((owners, 128), BF16)
        blocks = dot((block_hot * iota((owners, rows), 0).astype(F32)).astype(BF16), ones, 0, 0)
        slot_col = blocks * PAD + dot(counts.astype(BF16), ones, 0, 0)
        for j in range(owners * PAD // 128):
            back_place[:, 128 * j : 128 * j + 128] = hot(
                (iota((rows, 128), 1) + 128 * j).astype(F32) == slot_col
            ).astype(BF16)
    ag_step(3)
    with scope("cotangents_wait"):
        for d in range(1, NM):
            ref = ua.at[:, lanes(lax.rem(m + NM - d, NM))]
            remote(ref, ref, u_s.at[d], u_r.at[d], m_peer(d)).wait_recv()
    ag_step(4)
    with scope("base_gradient"):
        for j in range(2):
            fg[256 * j : 256 * j + 256] = dot(ua[256 * j : 256 * j + 256], w[...], 1, 1)
    ag_step(5)

    lane = iota((NY * PAD, 128), 1) < 64

    def masks(k):
        v = rbuf[k, :, feats:].astype(F32).reshape(NY, PAD, 128)[:, PAD - 1 :, :]
        return jnp.broadcast_to(v, (NY, PAD, 128)).reshape(NY * PAD, 128)

    def rows_wait():
        with scope("rows_wait"):
            own.wait()
            for d in range(1, NY):
                ref = rbuf.at[:, pl.ds(pl.multiple_of(lax.rem(yi + NY - d, NY) * PAD, PAD), PAD), :]
                remote(ref, ref, y_s.at[d], y_r.at[d], y_peer(d)).wait_recv()

    def first(k):
        mask = masks(k)
        inner = dot(rbuf[k, :, :feats], panels[k, :, :feats], 1, 1) * mask
        back = dot(rbuf[k, :, feats:], panels[k, :, feats:], 1, 1) * mask
        inner = inner + pltpu.roll(inner, 64, 1)
        back = back + pltpu.roll(back, 64, 1)
        pk[k] = jnp.where(lane, inner, back)

    def x_send(b):
        k0, k1 = BATCHES[b]
        for d in range(1, NM):
            p = lax.rem(m + d, NM)
            go(pk.at[k0:k1, pl.ds(pl.multiple_of(p * 8, 8), 8), :], rsr.at[m, k0:k1],
               xs_s.at[b, d], xs_r.at[b, d], m_peer(d))

    def x_reduce(b):
        k0, k1 = BATCHES[b]
        mine = pl.ds(pl.multiple_of(m * 8, 8), 8)
        acc = pk[k0:k1, mine, :]
        for d in range(1, NM):
            src = lax.rem(m + NM - d, NM)
            ref = rsr.at[src, k0:k1]
            remote(ref, ref, xs_s.at[b, d], xs_r.at[b, d], m_peer(d)).wait_recv()
            acc = acc + rsr[src, k0:k1]
        pkf[k0:k1, mine, :] = acc.astype(BF16).astype(F32)
        for d in range(1, NM):
            ref = pkf.at[k0:k1, mine, :]
            go(ref, ref, xg_s.at[b, d], xg_r.at[b, d], m_peer(d))

    def x_finish(b):
        k0, k1 = BATCHES[b]
        for d in range(1, NM):
            src = lax.rem(m + NM - d, NM)
            ref = pkf.at[k0:k1, pl.ds(pl.multiple_of(src * 8, 8), 8), :]
            remote(ref, ref, xg_s.at[b, d], xg_r.at[b, d], m_peer(d)).wait_recv()

    def spread(k):
        mask = masks(k)
        v = pkf[k]
        r = pltpu.roll(v, 64, 1)
        return (jnp.where(lane, v, r) * mask).astype(BF16), (jnp.where(lane, r, v) * mask).astype(BF16)

    def sums(k):
        inner, back = spread(k)
        part[k, :, :feats] = dot(back, rbuf[k, :, :feats], 0, 0)
        part[k, :, feats:] = dot(inner, rbuf[k, :, feats:], 0, 0)

    def rows_back(k):
        inner, back = spread(k)
        grad = (SCALE * dot(back, panels[k, :, :feats], 1, 0)).astype(BF16)
        delta = (SCALE * dot(inner, panels[k, :, feats:], 1, 0)).astype(BF16)
        for q in range(NY):
            rets[q, k, :, :feats] = grad[q * PAD : (q + 1) * PAD]
            rets[q, k, :, feats:] = delta[q * PAD : (q + 1) * PAD]

    locals_ = [own]

    def ret_send(i, k0, k1):
        for d in range(1, NY):
            go(rets.at[lax.rem(yi + d, NY), k0:k1], ret.at[yi, k0:k1], rt_s.at[i, d], rt_r.at[i, d], y_peer(d))
        c = pltpu.make_async_copy(rets.at[yi, k0:k1], ret.at[yi, k0:k1], loc.at[1 + i])
        c.start()
        locals_.append(c)

    def ret_wait(i, k0, k1):
        locals_[1 + i].wait()
        for d in range(1, NY):
            ref = ret.at[lax.rem(yi + NY - d, NY), k0:k1]
            remote(ref, ref, rt_s.at[i, d], rt_r.at[i, d], y_peer(d)).wait_recv()

    for c in range(6, 9):
        ag_step(c)
    rows_wait()
    with scope("ranks_0"):
        for k in range(3):
            first(k)
    ag_step(9)
    with scope("ranks_1"):
        for k in range(3, 6):
            first(k)
    ag_step(10)
    with scope("ranks_2"):
        for k in range(6, 9):
            first(k)
        x_send(0)
    ag_step(11)
    with scope("ranks_3"):
        first(9)
        first(10)
    with scope("reduce_0"):
        x_reduce(0)
    ag_step(12)
    with scope("ranks_4"):
        first(11)
        first(12)
        x_send(1)
    with scope("finish_0"):
        x_finish(0)
    rows_back(0)
    ag_step(13)
    with scope("ranks_5"):
        first(13)
        first(14)
    with scope("reduce_1"):
        x_reduce(1)
    ag_step(14)
    with scope("ranks_6"):
        first(15)
        x_send(2)
    with scope("finish_1"):
        x_finish(1)
    with scope("rows_back_a"):
        for k in range(1, 5):
            rows_back(k)
    with scope("reduce_2"):
        x_reduce(2)
    with scope("rows_back_b"):
        for k in range(5, 8):
            rows_back(k)
        ret_send(0, 0, 8)
    with scope("finish_2"):
        x_finish(2)

    def piece(w, c):
        s, h = FAR - (c + 1) // 2, (c % 2 if c else 0)
        hh = h if w == 0 else 1 - h
        return (above(s) if w == 0 else below(s)), pl.ds(half * hh, half)

    def rs_step(c):
        with scope(f"sum_hop_{c}"):
            for v, dev in enumerate((up, down)):
                k, part_rows = piece(v, c)
                x = part[k, part_rows, :]
                if c >= 2:
                    ref = prec.at[v, c - 2]
                    remote(ref, ref, rs_s.at[v, c - 2], rs_r.at[v, c - 2], dev).wait_recv()
                    x = x + prec[v, c - 2].astype(F32)
                psend[v, c] = x.astype(BF16)
                go(psend.at[v, c], prec.at[v, c], rs_s.at[v, c], rs_r.at[v, c], dev)

    sums(15)
    rs_step(0)
    sums(14)
    sums(13)
    rs_step(1)
    rows_back(8)
    rows_back(9)
    rs_step(2)
    for i, s in enumerate(range(6, 0, -1)):
        with scope("sums"):
            sums(2 * s)
            sums(2 * s - 1)
        rs_step(3 + 2 * i)
        if i < 3:
            with scope("rows_back_c"):
                rows_back(10 + 2 * i)
                rows_back(11 + 2 * i)
        if i == 2:
            ret_send(1, 8, 16)
        if i == 3:
            with scope("base_wait"):
                acc = fs[m]
                for d in range(1, NM):
                    src = lax.rem(m + NM - d, NM)
                    remote(fr.at[src], fr.at[src], f_s.at[d], f_r.at[d], m_peer(d)).wait_recv()
                    acc = acc + fr[src]
                fs[m] = acc
        rs_step(4 + 2 * i)
    sums(0)
    with scope("returned_wait"):
        ret_wait(0, 0, 8)
        ret_wait(1, 8, 16)
    with scope("outputs"):
        mine = ret[...].reshape(NY * NZ * PAD, wide)
        for j in range(4):
            r = pl.ds(128 * j, 128)
            place = back_place[r]
            tig_ref[r] = (fg[r] + dot(place, mine[:, :feats], 1, 0)).astype(BF16)
            proj_ref[r] = (fs[m, r] + dot(place, mine[:, feats:], 1, 0)).astype(BF16)
    with scope("last_sums"):
        for v, dev in enumerate((up, down)):
            for c in (CHUNKS - 2, CHUNKS - 1):
                ref = prec.at[v, c]
                remote(ref, ref, rs_s.at[v, c], rs_r.at[v, c], dev).wait_recv()
        for p in range(2):
            scale = SCALE * (1 - flags_ref[p]).astype(F32)
            c0, c1 = (CHUNKS - 1, CHUNKS - 2) if p == 0 else (CHUNKS - 2, CHUNKS - 1)
            r = slice(p * half, (p + 1) * half)
            v = scale * (part[0, r] + prec[0, c0].astype(F32) + prec[1, c1].astype(F32))
            down_ref[r] = v[:, :feats].astype(BF16)
            upg_ref[r] = v[:, feats:].astype(BF16)
    with scope("sent"):
        for c in started:
            c.wait_send()


def fused(tokens, weight, at, b, ids, panel_of, flags, upstream):
    rows, feats = tokens.shape
    n = at.shape[0]
    half = n // 2
    wide = feats + 128
    vm = pl.BlockSpec(memory_space=pltpu.VMEM)
    hbm = pl.BlockSpec(memory_space=pl.ANY)
    dma = pltpu.SemaphoreType.DMA
    group = NY * PAD
    nb = len(BATCHES)
    return pl.pallas_call(
        kernel,
        out_shape=(
            jax.ShapeDtypeStruct((rows, 128), BF16),
            jax.ShapeDtypeStruct((rows, feats), BF16),
            jax.ShapeDtypeStruct((n, feats), BF16),
            jax.ShapeDtypeStruct((n, 128), BF16),
        ),
        in_specs=[hbm, hbm, vm, vm, vm, vm, pl.BlockSpec(memory_space=pltpu.SMEM), vm],
        out_specs=(vm, vm, vm, vm),
        scratch_shapes=[
            pltpu.VMEM((rows, feats), BF16),
            pltpu.VMEM(weight.shape, BF16),
            pltpu.VMEM((rows, NM * 128), BF16),
            pltpu.VMEM((NM, rows, 128), F32),
            pltpu.VMEM((NM, rows, 128), F32),
            pltpu.VMEM((rows, feats), F32),
            pltpu.VMEM((rows, NY * NZ * PAD), BF16),
            pltpu.VMEM((NY, NZ, PAD, wide), BF16),
            pltpu.VMEM((NY, NZ, PAD, wide), BF16),
            pltpu.VMEM((NZ, n, wide), BF16),
            pltpu.VMEM((NZ, group, wide), BF16),
            pltpu.VMEM((NY, NZ, PAD, wide), BF16),
            pltpu.VMEM((NZ, group, 128), F32),
            pltpu.VMEM((NM, NZ, group // NM, 128), F32),
            pltpu.VMEM((NZ, group, 128), F32),
            pltpu.VMEM((NZ, n, wide), F32),
            pltpu.VMEM((2, CHUNKS, half, wide), BF16),
            pltpu.VMEM((2, CHUNKS, half, wide), BF16),
            dma((2, CHUNKS)), dma((2, CHUNKS)),
            dma((NY,)), dma((NY,)),
            dma((2, NY)), dma((2, NY)),
            dma((nb, NM)), dma((nb, NM)),
            dma((nb, NM)), dma((nb, NM)),
            dma((2, CHUNKS)), dma((2, CHUNKS)),
            dma((NM,)), dma((NM,)),
            dma((NM,)), dma((NM,)),
            dma((5,)),
        ],
        compiler_params=pltpu.CompilerParams(
            collective_id=0, has_side_effects=True, vmem_limit_bytes=58 * 2**20
        ),
        cost_estimate=pl.CostEstimate(flops=5 * 10**9, bytes_accessed=10**7, transcendentals=0),
    )(tokens, weight, at, b, ids, panel_of, flags, upstream)


def shards(tokens, base_weight, adapter_a, adapter_b, row_ids, panel_of, stop_flags, upstream):
    per_owner, feats, rank = adapter_a.shape
    vals = upstream.shape[1]
    at = jnp.transpose(adapter_a, (0, 2, 1)).reshape(per_owner * rank, feats)
    b = adapter_b.reshape(per_owner * rank, vals)
    projected, gradient, down, up = fused(
        tokens, base_weight, at, b, row_ids.reshape(1, -1), panel_of.reshape(1, -1), stop_flags, upstream
    )
    return (
        projected,
        gradient,
        jnp.transpose(down.reshape(per_owner, rank, feats), (0, 2, 1)),
        up.reshape(per_owner, rank, vals),
    )


def solution(mesh):
    fine = Mesh(mesh.devices.reshape(NY, NZ, NX, NC), ("y", "z", "x", "core"))
    placed = (
        P(DP, MP),
        P(MP, None),
        P(DP, MP, None),
        P(DP, None, MP),
        P(DP),
        P(),
        P(DP),
        P(DP, MP),
    )
    return jax.shard_map(
        shards,
        mesh=fine,
        in_specs=placed,
        out_specs=(P(DP, MP), P(DP, MP), P(DP, MP, None), P(DP, None, MP)),
        check_vma=False,
    )
```

```python
import jax
import jax.numpy as jnp
from jax import lax
from jax.experimental import pallas as pl
from jax.experimental.pallas import tpu as pltpu
from jax.sharding import Mesh
from jax.sharding import PartitionSpec as P

SCALE = 2.0
F32 = jnp.float32
BF16 = jnp.bfloat16
NY, NZ, NX, NC = 4, 16, 4, 2
NM = NX * NC
PAD = 16
FAR = NZ // 2
DP = ("y", "z")
MP = ("x", "core")
BATCHES = ((0, 9), (9, 13), (13, 15))
CHUNKS = 2 * FAR - 1


def dot(a, b, ca, cb):
    return lax.dot_general(a, b, (((ca,), (cb,)), ((), ())), preferred_element_type=F32)


def below(s):
    return 0 if s == 0 else (NZ - 1 if s == FAR else 2 * s - 1)


def above(s):
    return 0 if s == 0 else (NZ - 1 if s == FAR else 2 * s)


def kernel(tok_hbm, w_hbm, at_ref, b_ref, ids_ref, panel_ref, flags_ref, up_ref,
           proj_ref, tig_ref, down_ref, upg_ref,
           tok, w, ua, fs, fr, fg, back_place, send, ret, panels, rbuf, rets, pk, rsr, pkf, whole, proj, part, psend, prec,
           ag_s, ag_r, y_s, y_r, rt_s, rt_r, xs_s, xs_r, xg_s, xg_r, rs_s, rs_r, u_s, u_r, f_s, f_r, b_s, b_r, loc):
    scope = jax.named_scope
    rows, feats = tok.shape
    wide = feats + 128
    half = at_ref.shape[0] // 2
    yi, zi, xi, ci = (lax.axis_index(n) for n in ("y", "z", "x", "core"))
    m = xi * NC + ci
    up = {"z": lax.rem(zi + 1, NZ)}
    down = {"z": lax.rem(zi + NZ - 1, NZ)}

    def y_peer(d):
        return {"y": lax.rem(yi + d, NY)}

    def m_peer(d):
        p = lax.rem(m + d, NM)
        return {"x": p // NC, "core": lax.rem(p, NC)}

    def lanes(p):
        return pl.ds(pl.multiple_of(p * 128, 128), 128)

    tok_in = pltpu.make_async_copy(tok_hbm, tok, loc.at[3])
    tok_in.start()
    w_in = pltpu.make_async_copy(w_hbm, w, loc.at[4])
    w_in.start()
    with scope("entry"):
        bar = pltpu.get_barrier_semaphore()
        peers = [up, down] + [y_peer(d) for d in range(1, NY)] + [m_peer(d) for d in range(1, NM)]
        for p in peers:
            pl.semaphore_signal(bar, inc=1, device_id=p, device_id_type=pl.DeviceIdType.MESH)
        panels[0, :, :feats] = at_ref[...]
        panels[0, :, feats:] = b_ref[...]
        pl.semaphore_wait(bar, len(peers))

    started = []

    def remote(src, dst, ssem, rsem, dev):
        return pltpu.make_async_remote_copy(
            src_ref=src, dst_ref=dst, send_sem=ssem, recv_sem=rsem, device_id=dev,
            device_id_type=pl.DeviceIdType.MESH,
        )

    def go(*a):
        c = remote(*a)
        c.start()
        started.append(c)

    def ag_start(c):
        s, h = c // 2, c % 2
        for v, (dev, here, there) in enumerate(
            ((up, below(s), below(s + 1)), (down, above(s), above(s + 1)))
        ):
            part_rows = pl.ds(half * (h if v == 0 else 1 - h), half)
            go(panels.at[here, part_rows], panels.at[there, part_rows], ag_s.at[v, c], ag_r.at[v, c], dev)

    def ag_step(c):
        s, h = c // 2, c % 2
        with scope(f"panel_hop_{c}"):
            for v, (dev, there) in enumerate(((up, below(s + 1)), (down, above(s + 1)))):
                ref = panels.at[there, pl.ds(half * (h if v == 0 else 1 - h), half)]
                remote(ref, ref, ag_s.at[v, c], ag_r.at[v, c], dev).wait_recv()
            if c + 2 < CHUNKS:
                ag_start(c + 2)

    ag_start(0)
    ag_start(1)

    def iota(shape, d):
        return lax.broadcasted_iota(jnp.int32, shape, d)

    def hot(cond):
        return jnp.where(cond, 1.0, 0.0)

    with scope("routing"):
        n_panels = panel_ref.shape[1]
        owners = NY * NZ
        rank = 64
        named = hot(iota((n_panels, rows), 0) == ids_ref[...]).astype(BF16)
        mapped = hot(iota((n_panels, n_panels), 0) == panel_ref[...]).astype(BF16)
        panel_hot = dot(mapped, named, 1, 0)
        panel = jnp.sum(panel_hot * iota((n_panels, rows), 0).astype(F32), axis=0, keepdims=True).astype(jnp.int32)
        owner = panel // 2
        within = panel - owner * 2
        own_y = owner // NZ
        away = owner - own_y * NZ - zi
        away = jnp.where(away < 0, away + NZ, away)
        order = jnp.where(away == FAR, NZ - 1, jnp.where(away < FAR, 2 * away, 2 * (NZ - away) - 1))
        block = own_y * NZ + order
        block_hot = hot(iota((owners, rows), 0) == block)
        before = hot(iota((rows, rows), 0) < iota((rows, rows), 1)).astype(BF16)
        counts = dot(block_hot.astype(BF16), before, 1, 0) * block_hot
        earlier = jnp.sum(counts, axis=0, keepdims=True).astype(jnp.int32)
        slot = block * PAD + earlier
        which = jnp.max(block_hot * within.astype(F32), axis=1, keepdims=True)
        pick = hot((iota((owners, 128), 1) // rank).astype(F32) == which)
        last = iota((NZ * PAD, 128), 0) % PAD == PAD - 1
        tok_in.wait()
    with scope("rows_out"):
        for q in range(NY):
            place = hot(iota((NZ * PAD, rows), 0) + q * NZ * PAD == slot).astype(BF16)
            t = dot(place, tok[...], 1, 0).astype(BF16)
            u = dot(place, up_ref[...], 1, 0)
            marks = jnp.broadcast_to(pick[q * NZ : (q + 1) * NZ].reshape(NZ, 1, 128), (NZ, PAD, 128))
            u = jnp.where(last, marks.reshape(NZ * PAD, 128), u).astype(BF16)
            send[q, :, :, :feats] = t.reshape(NZ, PAD, feats)
            send[q, :, :, feats:] = u.reshape(NZ, PAD, 128)
        mine_rows = pl.ds(pl.multiple_of(yi * PAD, PAD), PAD)
        for d in range(1, NY):
            go(send.at[lax.rem(yi + d, NY)], rbuf.at[:, mine_rows, :], y_s.at[d], y_r.at[d], y_peer(d))
        own = pltpu.make_async_copy(send.at[yi], rbuf.at[:, mine_rows, :], loc.at[0])
        own.start()
    ag_step(0)
    with scope("cotangents_out"):
        for d in range(1, NM):
            go(up_ref, ua.at[:, lanes(m)], u_s.at[d], u_r.at[d], m_peer(d))
        ua[:, lanes(m)] = up_ref[...]
        w_in.wait()
    with scope("base"):
        for j in range(NM // 2):
            r = dot(tok[...], w[:, 256 * j : 256 * j + 256], 1, 0)
            fs[2 * j] = r[:, :128]
            fs[2 * j + 1] = r[:, 128:]
    ag_step(1)
    with scope("base_out"):
        for d in range(1, NM):
            p = lax.rem(m + d, NM)
            go(fs.at[p], fr.at[m], f_s.at[d], f_r.at[d], m_peer(d))
    ag_step(2)
    with scope("row_places"):
        ones = jnp.ones((owners, 128), BF16)
        blocks = dot((block_hot * iota((owners, rows), 0).astype(F32)).astype(BF16), ones, 0, 0)
        slot_col = blocks * PAD + dot(counts.astype(BF16), ones, 0, 0)
        for j in range(owners * PAD // 128):
            back_place[:, 128 * j : 128 * j + 128] = hot(
                (iota((rows, 128), 1) + 128 * j).astype(F32) == slot_col
            ).astype(BF16)
    ag_step(3)
    with scope("cotangents_wait"):
        for d in range(1, NM):
            ref = ua.at[:, lanes(lax.rem(m + NM - d, NM))]
            remote(ref, ref, u_s.at[d], u_r.at[d], m_peer(d)).wait_recv()
    ag_step(4)
    with scope("base_gradient"):
        for j in range(2):
            fg[256 * j : 256 * j + 256] = dot(ua[256 * j : 256 * j + 256], w[...], 1, 1)
    ag_step(5)

    lane = iota((NY * PAD, 128), 1) < 64

    def masks(k):
        v = rbuf[k, :, feats:].astype(F32).reshape(NY, PAD, 128)[:, PAD - 1 :, :]
        return jnp.broadcast_to(v, (NY, PAD, 128)).reshape(NY * PAD, 128)

    def rows_wait():
        with scope("rows_wait"):
            own.wait()
            for d in range(1, NY):
                ref = rbuf.at[:, pl.ds(pl.multiple_of(lax.rem(yi + NY - d, NY) * PAD, PAD), PAD), :]
                remote(ref, ref, y_s.at[d], y_r.at[d], y_peer(d)).wait_recv()

    def first(k):
        mask = masks(k)
        inner = dot(rbuf[k, :, :feats], panels[k, :, :feats], 1, 1) * mask
        back = dot(rbuf[k, :, feats:], panels[k, :, feats:], 1, 1) * mask
        inner = inner + pltpu.roll(inner, 64, 1)
        back = back + pltpu.roll(back, 64, 1)
        pk[k] = jnp.where(lane, inner, back)

    def x_send(b):
        k0, k1 = BATCHES[b]
        for d in range(1, NM):
            p = lax.rem(m + d, NM)
            go(pk.at[k0:k1, pl.ds(pl.multiple_of(p * 8, 8), 8), :], rsr.at[m, k0:k1],
               xs_s.at[b, d], xs_r.at[b, d], m_peer(d))

    def x_reduce(b):
        k0, k1 = BATCHES[b]
        mine = pl.ds(pl.multiple_of(m * 8, 8), 8)
        acc = pk[k0:k1, mine, :]
        for d in range(1, NM):
            src = lax.rem(m + NM - d, NM)
            ref = rsr.at[src, k0:k1]
            remote(ref, ref, xs_s.at[b, d], xs_r.at[b, d], m_peer(d)).wait_recv()
            acc = acc + rsr[src, k0:k1]
        pkf[k0:k1, mine, :] = acc.astype(BF16).astype(F32)
        for d in range(1, NM):
            ref = pkf.at[k0:k1, mine, :]
            go(ref, ref, xg_s.at[b, d], xg_r.at[b, d], m_peer(d))

    def x_finish(b):
        k0, k1 = BATCHES[b]
        for d in range(1, NM):
            src = lax.rem(m + NM - d, NM)
            ref = pkf.at[k0:k1, pl.ds(pl.multiple_of(src * 8, 8), 8), :]
            remote(ref, ref, xg_s.at[b, d], xg_r.at[b, d], m_peer(d)).wait_recv()

    def spread(k):
        mask = masks(k)
        v = pkf[k]
        r = pltpu.roll(v, 64, 1)
        return (jnp.where(lane, v, r) * mask).astype(BF16), (jnp.where(lane, r, v) * mask).astype(BF16)

    def sums(k):
        inner, back = spread(k)
        part[k, :, :feats] = dot(back, rbuf[k, :, :feats], 0, 0)
        part[k, :, feats:] = dot(inner, rbuf[k, :, feats:], 0, 0)

    def rows_back(k):
        inner, back = spread(k)
        grad = (SCALE * dot(back, panels[k, :, :feats], 1, 0)).astype(BF16)
        delta = (SCALE * dot(inner, panels[k, :, feats:], 1, 0)).astype(BF16)
        for q in range(NY):
            rets[q, k, :, :feats] = grad[q * PAD : (q + 1) * PAD]
            rets[q, k, :, feats:] = delta[q * PAD : (q + 1) * PAD]

    locals_ = [own]

    def ret_send(i, k0, k1):
        for d in range(1, NY):
            go(rets.at[lax.rem(yi + d, NY), k0:k1], ret.at[yi, k0:k1], rt_s.at[i, d], rt_r.at[i, d], y_peer(d))
        c = pltpu.make_async_copy(rets.at[yi, k0:k1], ret.at[yi, k0:k1], loc.at[1 + i])
        c.start()
        locals_.append(c)

    def ret_wait(i, k0, k1):
        locals_[1 + i].wait()
        for d in range(1, NY):
            ref = ret.at[lax.rem(yi + NY - d, NY), k0:k1]
            remote(ref, ref, rt_s.at[i, d], rt_r.at[i, d], y_peer(d)).wait_recv()

    for c in range(6, 9):
        ag_step(c)
    rows_wait()
    with scope("ranks_0"):
        for k in range(3):
            first(k)
    ag_step(9)
    with scope("ranks_1"):
        for k in range(3, 6):
            first(k)
    ag_step(10)
    with scope("ranks_2"):
        for k in range(6, 9):
            first(k)
        x_send(0)
    ag_step(11)
    with scope("ranks_3"):
        first(9)
        first(10)
    with scope("reduce_0"):
        x_reduce(0)
    ag_step(12)
    with scope("ranks_4"):
        first(11)
        first(12)
        x_send(1)
    with scope("finish_0"):
        x_finish(0)
    rows_back(0)
    ag_step(13)
    with scope("ranks_5"):
        first(13)
        first(14)
        x_send(2)
    with scope("reduce_1"):
        x_reduce(1)
    ag_step(14)
    with scope("ranks_6"):
        first(15)
        for d in range(1, NM):
            go(pk.at[15], whole.at[m], b_s.at[d], b_r.at[d], m_peer(d))
        whole[m] = pk[15]
    with scope("reduce_2"):
        x_reduce(2)
    with scope("rows_back_a"):
        for k in range(1, 5):
            rows_back(k)
    with scope("finish_last"):
        for d in range(1, NM):
            ref = whole.at[lax.rem(m + NM - d, NM)]
            remote(ref, ref, b_s.at[d], b_r.at[d], m_peer(d)).wait_recv()
        pkf[15] = sum(whole[j] for j in range(NM)).astype(BF16).astype(F32)

    def piece(w, c):
        s, h = FAR - (c + 1) // 2, (c % 2 if c else 0)
        hh = h if w == 0 else 1 - h
        return (above(s) if w == 0 else below(s)), pl.ds(half * hh, half)

    def rs_step(c):
        with scope(f"sum_hop_{c}"):
            for v, dev in enumerate((up, down)):
                k, part_rows = piece(v, c)
                x = part[k, part_rows, :]
                if c >= 2:
                    ref = prec.at[v, c - 2]
                    remote(ref, ref, rs_s.at[v, c - 2], rs_r.at[v, c - 2], dev).wait_recv()
                    x = x + prec[v, c - 2].astype(F32)
                psend[v, c] = x.astype(BF16)
                go(psend.at[v, c], prec.at[v, c], rs_s.at[v, c], rs_r.at[v, c], dev)

    sums(15)
    rs_step(0)
    with scope("finish_2"):
        x_finish(2)
    sums(14)
    sums(13)
    rs_step(1)
    with scope("finish_1"):
        x_finish(1)
    with scope("rows_back_b"):
        for k in range(5, 8):
            rows_back(k)
        ret_send(0, 0, 8)
    rs_step(2)
    for i, s in enumerate(range(6, 0, -1)):
        with scope("sums"):
            sums(2 * s)
            sums(2 * s - 1)
        rs_step(3 + 2 * i)
        if i < 4:
            with scope("rows_back_c"):
                rows_back(8 + 2 * i)
                rows_back(9 + 2 * i)
        if i == 3:
            ret_send(1, 8, 16)
        if i == 4:
            with scope("base_wait"):
                acc = fs[m]
                for d in range(1, NM):
                    src = lax.rem(m + NM - d, NM)
                    remote(fr.at[src], fr.at[src], f_s.at[d], f_r.at[d], m_peer(d)).wait_recv()
                    acc = acc + fr[src]
                fs[m] = acc
        rs_step(4 + 2 * i)
    sums(0)
    with scope("returned_wait"):
        ret_wait(0, 0, 8)
        ret_wait(1, 8, 16)
    with scope("outputs"):
        mine = ret[...].reshape(NY * NZ * PAD, wide)
        for j in range(4):
            r = pl.ds(128 * j, 128)
            place = back_place[r]
            ua[r] = (fg[r] + dot(place, mine[:, :feats], 1, 0)).astype(BF16)
            proj[r] = (fs[m, r] + dot(place, mine[:, feats:], 1, 0)).astype(BF16)
        tig_out = pltpu.make_async_copy(ua, tig_ref, loc.at[5])
        proj_out = pltpu.make_async_copy(proj, proj_ref, loc.at[6])
        tig_out.start()
        proj_out.start()
    with scope("last_sums"):
        for v, dev in enumerate((up, down)):
            for c in (CHUNKS - 2, CHUNKS - 1):
                ref = prec.at[v, c]
                remote(ref, ref, rs_s.at[v, c], rs_r.at[v, c], dev).wait_recv()
        for p in range(2):
            scale = SCALE * (1 - flags_ref[p]).astype(F32)
            c0, c1 = (CHUNKS - 1, CHUNKS - 2) if p == 0 else (CHUNKS - 2, CHUNKS - 1)
            r = slice(p * half, (p + 1) * half)
            v = scale * (part[0, r] + prec[0, c0].astype(F32) + prec[1, c1].astype(F32))
            down_ref[r] = v[:, :feats].astype(BF16)
            upg_ref[r] = v[:, feats:].astype(BF16)
    with scope("sent"):
        tig_out.wait()
        proj_out.wait()
        for c in started:
            c.wait_send()


def fused(tokens, weight, at, b, ids, panel_of, flags, upstream):
    rows, feats = tokens.shape
    n = at.shape[0]
    half = n // 2
    wide = feats + 128
    vm = pl.BlockSpec(memory_space=pltpu.VMEM)
    hbm = pl.BlockSpec(memory_space=pl.ANY)
    dma = pltpu.SemaphoreType.DMA
    group = NY * PAD
    nb = len(BATCHES)
    return pl.pallas_call(
        kernel,
        out_shape=(
            jax.ShapeDtypeStruct((rows, 128), BF16),
            jax.ShapeDtypeStruct((rows, feats), BF16),
            jax.ShapeDtypeStruct((n, feats), BF16),
            jax.ShapeDtypeStruct((n, 128), BF16),
        ),
        in_specs=[hbm, hbm, vm, vm, vm, vm, pl.BlockSpec(memory_space=pltpu.SMEM), vm],
        out_specs=(hbm, hbm, vm, vm),
        scratch_shapes=[
            pltpu.VMEM((rows, feats), BF16),
            pltpu.VMEM(weight.shape, BF16),
            pltpu.VMEM((rows, NM * 128), BF16),
            pltpu.VMEM((NM, rows, 128), F32),
            pltpu.VMEM((NM, rows, 128), F32),
            pltpu.VMEM((rows, feats), F32),
            pltpu.VMEM((rows, NY * NZ * PAD), BF16),
            pltpu.VMEM((NY, NZ, PAD, wide), BF16),
            pltpu.VMEM((NY, NZ, PAD, wide), BF16),
            pltpu.VMEM((NZ, n, wide), BF16),
            pltpu.VMEM((NZ, group, wide), BF16),
            pltpu.VMEM((NY, NZ, PAD, wide), BF16),
            pltpu.VMEM((NZ, group, 128), F32),
            pltpu.VMEM((NM, NZ, group // NM, 128), F32),
            pltpu.VMEM((NZ, group, 128), F32),
            pltpu.VMEM((NM, group, 128), F32),
            pltpu.VMEM((rows, 128), BF16),
            pltpu.VMEM((NZ, n, wide), F32),
            pltpu.VMEM((2, CHUNKS, half, wide), BF16),
            pltpu.VMEM((2, CHUNKS, half, wide), BF16),
            dma((2, CHUNKS)), dma((2, CHUNKS)),
            dma((NY,)), dma((NY,)),
            dma((2, NY)), dma((2, NY)),
            dma((nb, NM)), dma((nb, NM)),
            dma((nb, NM)), dma((nb, NM)),
            dma((2, CHUNKS)), dma((2, CHUNKS)),
            dma((NM,)), dma((NM,)),
            dma((NM,)), dma((NM,)),
            dma((NM,)), dma((NM,)),
            dma((7,)),
        ],
        compiler_params=pltpu.CompilerParams(
            collective_id=0, has_side_effects=True, vmem_limit_bytes=58 * 2**20
        ),
        cost_estimate=pl.CostEstimate(flops=5 * 10**9, bytes_accessed=10**7, transcendentals=0),
    )(tokens, weight, at, b, ids, panel_of, flags, upstream)


def copies(*refs):
    n = (len(refs) - 2) // 3
    ins, outs, bufs, (in_sems, out_sems) = refs[:n], refs[n : 2 * n], refs[2 * n : 3 * n], refs[3 * n :]
    parts = []
    for i in range(n):
        cuts = 4 if ins[i].shape[0] * ins[i].shape[1] > 2**18 else 1
        step = ins[i].shape[0] // cuts
        for j in range(cuts):
            r = pl.ds(step * j, step)
            k = len(parts)
            parts.append((
                pltpu.make_async_copy(ins[i].at[r], bufs[i].at[r], in_sems.at[k]),
                pltpu.make_async_copy(bufs[i].at[r], outs[i].at[r], out_sems.at[k]),
            ))
    for c, _ in parts:
        c.start()
    for c, d in parts:
        c.wait()
        d.start()
    for _, d in parts:
        d.wait()


def settle(arrays):
    hbm = pl.BlockSpec(memory_space=pl.ANY)
    dma = pltpu.SemaphoreType.DMA
    return pl.pallas_call(
        copies,
        out_shape=tuple(jax.ShapeDtypeStruct(a.shape, a.dtype) for a in arrays),
        in_specs=[hbm] * len(arrays),
        out_specs=(hbm,) * len(arrays),
        scratch_shapes=[pltpu.VMEM(a.shape, a.dtype) for a in arrays]
        + [dma((4 * len(arrays),)), dma((4 * len(arrays),))],
    )(*arrays)


def shards(tokens, base_weight, adapter_a, adapter_b, row_ids, panel_of, stop_flags, upstream):
    per_owner, feats, rank = adapter_a.shape
    vals = upstream.shape[1]
    at = jnp.transpose(adapter_a, (0, 2, 1)).reshape(per_owner * rank, feats)
    b = adapter_b.reshape(per_owner * rank, vals)
    projected, gradient, down, up = settle(fused(
        tokens, base_weight, at, b, row_ids.reshape(1, -1), panel_of.reshape(1, -1), stop_flags, upstream
    ))
    return (
        projected,
        gradient,
        jnp.transpose(down.reshape(per_owner, rank, feats), (0, 2, 1)),
        up.reshape(per_owner, rank, vals),
    )


def solution(mesh):
    fine = Mesh(mesh.devices.reshape(NY, NZ, NX, NC), ("y", "z", "x", "core"))
    placed = (
        P(DP, MP),
        P(MP, None),
        P(DP, MP, None),
        P(DP, None, MP),
        P(DP),
        P(),
        P(DP),
        P(DP, MP),
    )
    return jax.shard_map(
        shards,
        mesh=fine,
        in_specs=placed,
        out_specs=(P(DP, MP), P(DP, MP), P(DP, MP, None), P(DP, None, MP)),
        check_vma=False,
    )
```

```python
import jax
import jax.numpy as jnp
from jax import lax
from jax.experimental import pallas as pl
from jax.experimental.pallas import tpu as pltpu
from jax.sharding import Mesh
from jax.sharding import PartitionSpec as P

SCALE = 2.0
F32 = jnp.float32
BF16 = jnp.bfloat16
NY, NZ, NX, NC = 4, 16, 4, 2
NM = NX * NC
PAD = 16
FAR = NZ // 2
DP = ("y", "z")
MP = ("x", "core")
BATCHES = ((0, 9), (9, 13))
CHUNKS = 2 * FAR - 1
SUM_HOPS = FAR - 2
SUMS = 2 * SUM_HOPS


def dot(a, b, ca, cb):
    return lax.dot_general(a, b, (((ca,), (cb,)), ((), ())), preferred_element_type=F32)


def below(s):
    return 0 if s == 0 else (NZ - 1 if s == FAR else 2 * s - 1)


def above(s):
    return 0 if s == 0 else (NZ - 1 if s == FAR else 2 * s)


def kernel(tok_hbm, w_hbm, at_ref, b_ref, ids_ref, panel_ref, flags_ref, up_ref,
           proj_ref, tig_ref, down_ref, upg_ref,
           tok, w, ua, fs, fr, fg, back_place, send, ret, panels, rbuf, rets, pk, rsr, pkf, short, whole, far_rows, far_ranks, proj, part, psend, prec,
           ag_s, ag_r, y_s, y_r, rt_s, rt_r, xs_s, xs_r, xg_s, xg_r, rs_s, rs_r, u_s, u_r, f_s, f_r, b_s, b_r, fr_s, fr_r, fk_s, fk_r, loc):
    scope = jax.named_scope
    rows, feats = tok.shape
    wide = feats + 128
    half = at_ref.shape[0] // 2
    yi, zi, xi, ci = (lax.axis_index(n) for n in ("y", "z", "x", "core"))
    m = xi * NC + ci
    up = {"z": lax.rem(zi + 1, NZ)}
    down = {"z": lax.rem(zi + NZ - 1, NZ)}
    up2 = {"z": lax.rem(zi + 2, NZ)}
    down2 = {"z": lax.rem(zi + NZ - 2, NZ)}

    def y_peer(d):
        return {"y": lax.rem(yi + d, NY)}

    def m_peer(d):
        p = lax.rem(m + d, NM)
        return {"x": p // NC, "core": lax.rem(p, NC)}

    def lanes(p):
        return pl.ds(pl.multiple_of(p * 128, 128), 128)

    tok_in = pltpu.make_async_copy(tok_hbm, tok, loc.at[3])
    tok_in.start()
    w_in = pltpu.make_async_copy(w_hbm, w, loc.at[4])
    w_in.start()
    with scope("entry"):
        bar = pltpu.get_barrier_semaphore()
        peers = [up, down, up2, down2] + [y_peer(d) for d in range(1, NY)] + [m_peer(d) for d in range(1, NM)]
        for p in peers:
            pl.semaphore_signal(bar, inc=1, device_id=p, device_id_type=pl.DeviceIdType.MESH)
        panels[0, :, :feats] = at_ref[...]
        panels[0, :, feats:] = b_ref[...]
        pl.semaphore_wait(bar, len(peers))

    started = []

    def remote(src, dst, ssem, rsem, dev):
        return pltpu.make_async_remote_copy(
            src_ref=src, dst_ref=dst, send_sem=ssem, recv_sem=rsem, device_id=dev,
            device_id_type=pl.DeviceIdType.MESH,
        )

    def go(*a):
        c = remote(*a)
        c.start()
        started.append(c)

    def ag_start(c):
        s, h = c // 2, c % 2
        for v, (dev, here, there) in enumerate(
            ((up, below(s), below(s + 1)), (down, above(s), above(s + 1)))
        ):
            part_rows = pl.ds(half * (h if v == 0 else 1 - h), half)
            go(panels.at[here, part_rows], panels.at[there, part_rows], ag_s.at[v, c], ag_r.at[v, c], dev)

    def ag_step(c):
        s, h = c // 2, c % 2
        with scope(f"panel_hop_{c}"):
            for v, (dev, there) in enumerate(((up, below(s + 1)), (down, above(s + 1)))):
                ref = panels.at[there, pl.ds(half * (h if v == 0 else 1 - h), half)]
                remote(ref, ref, ag_s.at[v, c], ag_r.at[v, c], dev).wait_recv()
            if c + 2 < CHUNKS:
                ag_start(c + 2)

    ag_start(0)
    ag_start(1)

    def iota(shape, d):
        return lax.broadcasted_iota(jnp.int32, shape, d)

    def hot(cond):
        return jnp.where(cond, 1.0, 0.0)

    with scope("routing"):
        n_panels = panel_ref.shape[1]
        owners = NY * NZ
        rank = 64
        named = hot(iota((n_panels, rows), 0) == ids_ref[...]).astype(BF16)
        mapped = hot(iota((n_panels, n_panels), 0) == panel_ref[...]).astype(BF16)
        panel_hot = dot(mapped, named, 1, 0)
        panel = jnp.sum(panel_hot * iota((n_panels, rows), 0).astype(F32), axis=0, keepdims=True).astype(jnp.int32)
        owner = panel // 2
        within = panel - owner * 2
        own_y = owner // NZ
        away = owner - own_y * NZ - zi
        away = jnp.where(away < 0, away + NZ, away)
        order = jnp.where(away == FAR, NZ - 1, jnp.where(away < FAR, 2 * away, 2 * (NZ - away) - 1))
        block = own_y * NZ + order
        block_hot = hot(iota((owners, rows), 0) == block)
        before = hot(iota((rows, rows), 0) < iota((rows, rows), 1)).astype(BF16)
        counts = dot(block_hot.astype(BF16), before, 1, 0) * block_hot
        earlier = jnp.sum(counts, axis=0, keepdims=True).astype(jnp.int32)
        slot = block * PAD + earlier
        which = jnp.max(block_hot * within.astype(F32), axis=1, keepdims=True)
        pick = hot((iota((owners, 128), 1) // rank).astype(F32) == which)
        last = iota((NZ * PAD, 128), 0) % PAD == PAD - 1
        tok_in.wait()
    with scope("rows_out"):
        for q in range(NY):
            place = hot(iota((NZ * PAD, rows), 0) + q * NZ * PAD == slot).astype(BF16)
            t = dot(place, tok[...], 1, 0).astype(BF16)
            u = dot(place, up_ref[...], 1, 0)
            marks = jnp.broadcast_to(pick[q * NZ : (q + 1) * NZ].reshape(NZ, 1, 128), (NZ, PAD, 128))
            u = jnp.where(last, marks.reshape(NZ * PAD, 128), u).astype(BF16)
            send[q, :, :, :feats] = t.reshape(NZ, PAD, feats)
            send[q, :, :, feats:] = u.reshape(NZ, PAD, 128)
        mine_rows = pl.ds(pl.multiple_of(yi * PAD, PAD), PAD)
        for d in range(1, NY):
            go(send.at[lax.rem(yi + d, NY)], rbuf.at[:, mine_rows, :], y_s.at[d], y_r.at[d], y_peer(d))
        own = pltpu.make_async_copy(send.at[yi], rbuf.at[:, mine_rows, :], loc.at[0])
        own.start()
    ag_step(0)
    with scope("cotangents_out"):
        for d in range(1, NM):
            go(up_ref, ua.at[:, lanes(m)], u_s.at[d], u_r.at[d], m_peer(d))
        ua[:, lanes(m)] = up_ref[...]
        w_in.wait()
    with scope("base"):
        for j in range(NM // 2):
            r = dot(tok[...], w[:, 256 * j : 256 * j + 256], 1, 0)
            fs[2 * j] = r[:, :128]
            fs[2 * j + 1] = r[:, 128:]
    ag_step(1)
    with scope("base_out"):
        for d in range(1, NM):
            p = lax.rem(m + d, NM)
            go(fs.at[p], fr.at[m], f_s.at[d], f_r.at[d], m_peer(d))
    ag_step(2)
    with scope("row_places"):
        ones = jnp.ones((owners, 128), BF16)
        blocks = dot((block_hot * iota((owners, rows), 0).astype(F32)).astype(BF16), ones, 0, 0)
        slot_col = blocks * PAD + dot(counts.astype(BF16), ones, 0, 0)
        for j in range(owners * PAD // 128):
            back_place[:, 128 * j : 128 * j + 128] = hot(
                (iota((rows, 128), 1) + 128 * j).astype(F32) == slot_col
            ).astype(BF16)
    ag_step(3)
    with scope("cotangents_wait"):
        for d in range(1, NM):
            ref = ua.at[:, lanes(lax.rem(m + NM - d, NM))]
            remote(ref, ref, u_s.at[d], u_r.at[d], m_peer(d)).wait_recv()
    ag_step(4)
    with scope("base_gradient"):
        for j in range(2):
            fg[256 * j : 256 * j + 256] = dot(ua[256 * j : 256 * j + 256], w[...], 1, 1)
    ag_step(5)

    lane = iota((NY * PAD, 128), 1) < 64

    def masks_of(v):
        n = v.shape[0] // PAD
        v = v.astype(F32).reshape(n, PAD, 128)[:, PAD - 1 :, :]
        return jnp.broadcast_to(v, (n, PAD, 128)).reshape(n * PAD, 128)

    def masks(k):
        return masks_of(rbuf[k, :, feats:])

    def rows_wait():
        with scope("rows_wait"):
            own.wait()
            for d in range(1, NY):
                ref = rbuf.at[:, pl.ds(pl.multiple_of(lax.rem(yi + NY - d, NY) * PAD, PAD), PAD), :]
                remote(ref, ref, y_s.at[d], y_r.at[d], y_peer(d)).wait_recv()

    def first(k):
        mask = masks(k)
        inner = dot(rbuf[k, :, :feats], panels[k, :, :feats], 1, 1) * mask
        back = dot(rbuf[k, :, feats:], panels[k, :, feats:], 1, 1) * mask
        inner = inner + pltpu.roll(inner, 64, 1)
        back = back + pltpu.roll(back, 64, 1)
        pk[k] = jnp.where(lane, inner, back)

    def x_send(b):
        k0, k1 = BATCHES[b]
        for d in range(1, NM):
            p = lax.rem(m + d, NM)
            go(pk.at[k0:k1, pl.ds(pl.multiple_of(p * 8, 8), 8), :], rsr.at[m, k0:k1],
               xs_s.at[b, d], xs_r.at[b, d], m_peer(d))

    def x_reduce(b):
        k0, k1 = BATCHES[b]
        mine = pl.ds(pl.multiple_of(m * 8, 8), 8)
        acc = pk[k0:k1, mine, :]
        for d in range(1, NM):
            src = lax.rem(m + NM - d, NM)
            ref = rsr.at[src, k0:k1]
            remote(ref, ref, xs_s.at[b, d], xs_r.at[b, d], m_peer(d)).wait_recv()
            acc = acc + rsr[src, k0:k1]
        pkf[k0:k1, mine, :] = acc.astype(BF16).astype(F32)
        for d in range(1, NM):
            ref = pkf.at[k0:k1, mine, :]
            go(ref, ref, xg_s.at[b, d], xg_r.at[b, d], m_peer(d))

    def x_finish(b):
        k0, k1 = BATCHES[b]
        for d in range(1, NM):
            src = lax.rem(m + NM - d, NM)
            ref = pkf.at[k0:k1, pl.ds(pl.multiple_of(src * 8, 8), 8), :]
            remote(ref, ref, xg_s.at[b, d], xg_r.at[b, d], m_peer(d)).wait_recv()

    def spread_of(v, mask):
        left = iota(v.shape, 1) < 64
        r = pltpu.roll(v, 64, 1)
        return (jnp.where(left, v, r) * mask).astype(BF16), (jnp.where(left, r, v) * mask).astype(BF16)

    def spread(k):
        return spread_of(pkf[k], masks(k))

    def sums(k):
        inner, back = spread(k)
        part[k, :, :feats] = dot(back, rbuf[k, :, :feats], 0, 0)
        part[k, :, feats:] = dot(inner, rbuf[k, :, feats:], 0, 0)

    def rows_back(k):
        inner, back = spread(k)
        grad = (SCALE * dot(back, panels[k, :, :feats], 1, 0)).astype(BF16)
        delta = (SCALE * dot(inner, panels[k, :, feats:], 1, 0)).astype(BF16)
        for q in range(NY):
            rets[q, k, :, :feats] = grad[q * PAD : (q + 1) * PAD]
            rets[q, k, :, feats:] = delta[q * PAD : (q + 1) * PAD]

    def whole_send(i, j0, j1):
        for j in range(j0, j1):
            short[j] = pk[13 + j].astype(BF16)
            whole[m, j] = short[j]
        for d in range(1, NM):
            go(short.at[j0:j1], whole.at[m, j0:j1], b_s.at[i, d], b_r.at[i, d], m_peer(d))

    def whole_finish(i, j0, j1):
        for d in range(1, NM):
            ref = whole.at[lax.rem(m + NM - d, NM), j0:j1]
            remote(ref, ref, b_s.at[i, d], b_r.at[i, d], m_peer(d)).wait_recv()
        for j in range(j0, j1):
            total = sum(whole[p, j].astype(F32) for p in range(NM))
            pkf[13 + j] = total.astype(BF16).astype(F32)

    near = NY * PAD
    far = near // 2
    far_pieces = (
        (0, up, 14, pl.ds(0, near), pl.ds(0, near)),
        (0, down, 13, pl.ds(0, near), pl.ds(0, near)),
        (1, up2, 15, pl.ds(0, far), pl.ds(near, far)),
        (1, down2, 15, pl.ds(far, far), pl.ds(near, far)),
    )

    def far_rows_send():
        for i, (_, dev, k, src, dst) in enumerate(far_pieces):
            go(rbuf.at[k, src], far_rows.at[i % 2, dst], fr_s.at[i], fr_r.at[i], dev)

    def far_ranks_send(stage):
        for i, (at_stage, dev, k, src, dst) in enumerate(far_pieces):
            if at_stage == stage:
                go(pkf.at[k, src], far_ranks.at[i % 2, dst], fk_s.at[i], fk_r.at[i], dev)

    def far_sums():
        for i, (_, dev, k, src, dst) in enumerate(far_pieces):
            rows_ref, ranks_ref = far_rows.at[i % 2, dst], far_ranks.at[i % 2, dst]
            remote(rows_ref, rows_ref, fr_s.at[i], fr_r.at[i], dev).wait_recv()
            remote(ranks_ref, ranks_ref, fk_s.at[i], fk_r.at[i], dev).wait_recv()
        for v, k in enumerate((12, 11)):
            inner, back = spread_of(far_ranks[v], masks_of(far_rows[v, :, feats:]))
            part[k, :, :feats] += dot(back, far_rows[v, :, :feats], 0, 0)
            part[k, :, feats:] += dot(inner, far_rows[v, :, feats:], 0, 0)

    locals_ = [own]

    def ret_send(i, k0, k1):
        for d in range(1, NY):
            go(rets.at[lax.rem(yi + d, NY), k0:k1], ret.at[yi, k0:k1], rt_s.at[i, d], rt_r.at[i, d], y_peer(d))
        c = pltpu.make_async_copy(rets.at[yi, k0:k1], ret.at[yi, k0:k1], loc.at[1 + i])
        c.start()
        locals_.append(c)

    def ret_wait(i, k0, k1):
        locals_[1 + i].wait()
        for d in range(1, NY):
            ref = ret.at[lax.rem(yi + NY - d, NY), k0:k1]
            remote(ref, ref, rt_s.at[i, d], rt_r.at[i, d], y_peer(d)).wait_recv()

    for c in range(6, 9):
        ag_step(c)
    rows_wait()
    with scope("ranks_0"):
        for k in range(3):
            first(k)
    ag_step(9)
    with scope("ranks_1"):
        for k in range(3, 6):
            first(k)
    ag_step(10)
    with scope("ranks_2"):
        for k in range(6, 9):
            first(k)
        x_send(0)
    ag_step(11)
    with scope("ranks_3"):
        first(9)
        first(10)
    with scope("reduce_0"):
        x_reduce(0)
    ag_step(12)
    with scope("ranks_4"):
        first(11)
        first(12)
        x_send(1)
    with scope("finish_0"):
        x_finish(0)
    rows_back(0)
    ag_step(13)
    with scope("ranks_5"):
        first(13)
        first(14)
        whole_send(0, 0, 2)
    with scope("reduce_1"):
        x_reduce(1)
    ag_step(14)
    with scope("far_rows_out"):
        far_rows_send()
    with scope("ranks_6"):
        first(15)
        whole_send(1, 2, 3)
    with scope("whole_0"):
        whole_finish(0, 0, 2)
        far_ranks_send(0)
    with scope("finish_1"):
        x_finish(1)
        sums(12)
        sums(11)
    with scope("whole_1"):
        whole_finish(1, 2, 3)
        far_ranks_send(1)
    with scope("rows_back_a"):
        for k in range(1, 4):
            rows_back(k)
    with scope("far_sums"):
        far_sums()

    def piece(v, c):
        s, h = SUM_HOPS - c // 2, c % 2
        return (above(s) if v == 0 else below(s)), pl.ds(half * (h if v == 0 else 1 - h), half)

    def rs_step(c):
        with scope(f"sum_hop_{c}"):
            for v, dev in enumerate((up, down)):
                k, part_rows = piece(v, c)
                x = part[k, part_rows, :]
                if c >= 2:
                    ref = prec.at[v, c - 2]
                    remote(ref, ref, rs_s.at[v, c - 2], rs_r.at[v, c - 2], dev).wait_recv()
                    x = x + prec[v, c - 2].astype(F32)
                psend[v, c] = x.astype(BF16)
                go(psend.at[v, c], prec.at[v, c], rs_s.at[v, c], rs_r.at[v, c], dev)

    rs_step(0)
    rs_step(1)
    for i, s in enumerate(range(SUM_HOPS - 1, 0, -1)):
        with scope("sums"):
            sums(2 * s)
            sums(2 * s - 1)
        rs_step(2 + 2 * i)
        if i == 0:
            with scope("rows_back_b"):
                for k in range(4, 8):
                    rows_back(k)
                ret_send(0, 0, 8)
        if i in (1, 2):
            with scope("rows_back_c"):
                for k in range(4):
                    rows_back(4 + 4 * i + k)
                if i == 2:
                    ret_send(1, 8, 16)
        if i == 3:
            with scope("base_wait"):
                acc = fs[m]
                for d in range(1, NM):
                    src = lax.rem(m + NM - d, NM)
                    remote(fr.at[src], fr.at[src], f_s.at[d], f_r.at[d], m_peer(d)).wait_recv()
                    acc = acc + fr[src]
                fs[m] = acc
        rs_step(3 + 2 * i)
    sums(0)
    with scope("returned_wait"):
        ret_wait(0, 0, 8)
        ret_wait(1, 8, 16)
    with scope("outputs"):
        mine = ret[...].reshape(NY * NZ * PAD, wide)
        for j in range(4):
            r = pl.ds(128 * j, 128)
            place = back_place[r]
            ua[r] = (fg[r] + dot(place, mine[:, :feats], 1, 0)).astype(BF16)
            proj[r] = (fs[m, r] + dot(place, mine[:, feats:], 1, 0)).astype(BF16)
        tig_out = pltpu.make_async_copy(ua, tig_ref, loc.at[5])
        proj_out = pltpu.make_async_copy(proj, proj_ref, loc.at[6])
        tig_out.start()
        proj_out.start()
    with scope("last_sums"):
        for v, dev in enumerate((up, down)):
            for c in (SUMS - 2, SUMS - 1):
                ref = prec.at[v, c]
                remote(ref, ref, rs_s.at[v, c], rs_r.at[v, c], dev).wait_recv()
        for p in range(2):
            scale = SCALE * (1 - flags_ref[p]).astype(F32)
            c0, c1 = (SUMS - 2, SUMS - 1) if p == 0 else (SUMS - 1, SUMS - 2)
            r = slice(p * half, (p + 1) * half)
            v = scale * (part[0, r] + prec[0, c0].astype(F32) + prec[1, c1].astype(F32))
            down_ref[r] = v[:, :feats].astype(BF16)
            upg_ref[r] = v[:, feats:].astype(BF16)
    with scope("sent"):
        tig_out.wait()
        proj_out.wait()
        for c in started:
            c.wait_send()


def fused(tokens, weight, at, b, ids, panel_of, flags, upstream):
    rows, feats = tokens.shape
    n = at.shape[0]
    half = n // 2
    wide = feats + 128
    vm = pl.BlockSpec(memory_space=pltpu.VMEM)
    hbm = pl.BlockSpec(memory_space=pl.ANY)
    dma = pltpu.SemaphoreType.DMA
    group = NY * PAD
    nb = len(BATCHES)
    return pl.pallas_call(
        kernel,
        out_shape=(
            jax.ShapeDtypeStruct((rows, 128), BF16),
            jax.ShapeDtypeStruct((rows, feats), BF16),
            jax.ShapeDtypeStruct((n, feats), BF16),
            jax.ShapeDtypeStruct((n, 128), BF16),
        ),
        in_specs=[hbm, hbm, vm, vm, vm, vm, pl.BlockSpec(memory_space=pltpu.SMEM), vm],
        out_specs=(hbm, hbm, vm, vm),
        scratch_shapes=[
            pltpu.VMEM((rows, feats), BF16),
            pltpu.VMEM(weight.shape, BF16),
            pltpu.VMEM((rows, NM * 128), BF16),
            pltpu.VMEM((NM, rows, 128), F32),
            pltpu.VMEM((NM, rows, 128), F32),
            pltpu.VMEM((rows, feats), F32),
            pltpu.VMEM((rows, NY * NZ * PAD), BF16),
            pltpu.VMEM((NY, NZ, PAD, wide), BF16),
            pltpu.VMEM((NY, NZ, PAD, wide), BF16),
            pltpu.VMEM((NZ, n, wide), BF16),
            pltpu.VMEM((NZ, group, wide), BF16),
            pltpu.VMEM((NY, NZ, PAD, wide), BF16),
            pltpu.VMEM((NZ, group, 128), F32),
            pltpu.VMEM((NM, NZ, group // NM, 128), F32),
            pltpu.VMEM((NZ, group, 128), F32),
            pltpu.VMEM((3, group, 128), BF16),
            pltpu.VMEM((NM, 3, group, 128), BF16),
            pltpu.VMEM((2, group + group // 2, wide), BF16),
            pltpu.VMEM((2, group + group // 2, 128), F32),
            pltpu.VMEM((rows, 128), BF16),
            pltpu.VMEM((NZ, n, wide), F32),
            pltpu.VMEM((2, SUMS, half, wide), BF16),
            pltpu.VMEM((2, SUMS, half, wide), BF16),
            dma((2, CHUNKS)), dma((2, CHUNKS)),
            dma((NY,)), dma((NY,)),
            dma((2, NY)), dma((2, NY)),
            dma((nb, NM)), dma((nb, NM)),
            dma((nb, NM)), dma((nb, NM)),
            dma((2, SUMS)), dma((2, SUMS)),
            dma((NM,)), dma((NM,)),
            dma((NM,)), dma((NM,)),
            dma((2, NM)), dma((2, NM)),
            dma((4,)), dma((4,)),
            dma((4,)), dma((4,)),
            dma((7,)),
        ],
        compiler_params=pltpu.CompilerParams(
            collective_id=0, has_side_effects=True, vmem_limit_bytes=58 * 2**20
        ),
        cost_estimate=pl.CostEstimate(flops=5 * 10**9, bytes_accessed=10**7, transcendentals=0),
    )(tokens, weight, at, b, ids, panel_of, flags, upstream)


def copies(*refs):
    n = (len(refs) - 2) // 3
    ins, outs, bufs, (in_sems, out_sems) = refs[:n], refs[n : 2 * n], refs[2 * n : 3 * n], refs[3 * n :]
    parts = []
    for i in range(n):
        cuts = 4 if ins[i].shape[0] * ins[i].shape[1] > 2**18 else 1
        step = ins[i].shape[0] // cuts
        for j in range(cuts):
            r = pl.ds(step * j, step)
            k = len(parts)
            parts.append((
                pltpu.make_async_copy(ins[i].at[r], bufs[i].at[r], in_sems.at[k]),
                pltpu.make_async_copy(bufs[i].at[r], outs[i].at[r], out_sems.at[k]),
            ))
    for c, _ in parts:
        c.start()
    for c, d in parts:
        c.wait()
        d.start()
    for _, d in parts:
        d.wait()


def settle(arrays):
    hbm = pl.BlockSpec(memory_space=pl.ANY)
    dma = pltpu.SemaphoreType.DMA
    return pl.pallas_call(
        copies,
        out_shape=tuple(jax.ShapeDtypeStruct(a.shape, a.dtype) for a in arrays),
        in_specs=[hbm] * len(arrays),
        out_specs=(hbm,) * len(arrays),
        scratch_shapes=[pltpu.VMEM(a.shape, a.dtype) for a in arrays]
        + [dma((4 * len(arrays),)), dma((4 * len(arrays),))],
    )(*arrays)


def shards(tokens, base_weight, adapter_a, adapter_b, row_ids, panel_of, stop_flags, upstream):
    per_owner, feats, rank = adapter_a.shape
    vals = upstream.shape[1]
    at = jnp.transpose(adapter_a, (0, 2, 1)).reshape(per_owner * rank, feats)
    b = adapter_b.reshape(per_owner * rank, vals)
    projected, gradient, down, up = settle(fused(
        tokens, base_weight, at, b, row_ids.reshape(1, -1), panel_of.reshape(1, -1), stop_flags, upstream
    ))
    return (
        projected,
        gradient,
        jnp.transpose(down.reshape(per_owner, rank, feats), (0, 2, 1)),
        up.reshape(per_owner, rank, vals),
    )


def solution(mesh):
    fine = Mesh(mesh.devices.reshape(NY, NZ, NX, NC), ("y", "z", "x", "core"))
    placed = (
        P(DP, MP),
        P(MP, None),
        P(DP, MP, None),
        P(DP, None, MP),
        P(DP),
        P(),
        P(DP),
        P(DP, MP),
    )
    return jax.shard_map(
        shards,
        mesh=fine,
        in_specs=placed,
        out_specs=(P(DP, MP), P(DP, MP), P(DP, MP, None), P(DP, None, MP)),
        check_vma=False,
    )
```

```python
import jax
import jax.numpy as jnp
from jax import lax
from jax.experimental import pallas as pl
from jax.experimental.pallas import tpu as pltpu
from jax.sharding import Mesh
from jax.sharding import PartitionSpec as P

SCALE = 2.0
F32 = jnp.float32
BF16 = jnp.bfloat16
NY, NZ, NX, NC = 4, 16, 4, 2
NM = NX * NC
PAD = 16
FAR = NZ // 2
DP = ("y", "z")
MP = ("x", "core")
BATCHES = ((0, 9), (9, 13))
CHUNKS = 2 * FAR - 1
SUM_HOPS = FAR - 2
SUMS = 2 * SUM_HOPS


def dot(a, b, ca, cb):
    return lax.dot_general(a, b, (((ca,), (cb,)), ((), ())), preferred_element_type=F32)


def below(s):
    return 0 if s == 0 else (NZ - 1 if s == FAR else 2 * s - 1)


def above(s):
    return 0 if s == 0 else (NZ - 1 if s == FAR else 2 * s)


def kernel(tok_hbm, w_hbm, at_hbm, b_hbm, ids_hbm, panel_hbm, flags_ref, up_hbm,
           proj_ref, tig_ref, down_ref, upg_ref,
           tok, w, ids_ref, panel_ref, up_ref, ua, fs, fr, fg, back_place, send, ret, panels, rbuf, rets, pk, rsr, pkf, short, whole, far_rows, far_ranks, proj, part, psend, prec,
           ag_s, ag_r, y_s, y_r, rt_s, rt_r, xs_s, xs_r, xg_s, xg_r, rs_s, rs_r, u_s, u_r, f_s, f_r, b_s, b_r, fr_s, fr_r, fk_s, fk_r, loc):
    scope = jax.named_scope
    rows, feats = tok.shape
    wide = feats + 128
    half = at_hbm.shape[0] // 2
    yi, zi, xi, ci = (lax.axis_index(n) for n in ("y", "z", "x", "core"))
    m = xi * NC + ci
    up = {"z": lax.rem(zi + 1, NZ)}
    down = {"z": lax.rem(zi + NZ - 1, NZ)}
    up2 = {"z": lax.rem(zi + 2, NZ)}
    down2 = {"z": lax.rem(zi + NZ - 2, NZ)}

    def y_peer(d):
        return {"y": lax.rem(yi + d, NY)}

    def m_peer(d):
        p = lax.rem(m + d, NM)
        return {"x": p // NC, "core": lax.rem(p, NC)}

    def lanes(p):
        return pl.ds(pl.multiple_of(p * 128, 128), 128)

    def load(src, dst, i):
        c = pltpu.make_async_copy(src, dst, loc.at[i])
        c.start()
        return c

    with scope("entry"):
        bar = pltpu.get_barrier_semaphore()
        peers = [up, down, up2, down2] + [y_peer(d) for d in range(1, NY)] + [m_peer(d) for d in range(1, NM)]
        for p in peers:
            pl.semaphore_signal(bar, inc=1, device_id=p, device_id_type=pl.DeviceIdType.MESH)
        panels_in = [
            load(at_hbm, panels.at[0, :, pl.ds(0, feats)], 7),
            load(b_hbm, panels.at[0, :, pl.ds(feats, 128)], 8),
        ]
        routes_in = [load(ids_hbm, ids_ref, 9), load(panel_hbm, panel_ref, 10), load(up_hbm, up_ref, 11)]
        tok_in = load(tok_hbm, tok, 3)
        w_in = load(w_hbm, w, 4)
        for c in panels_in:
            c.wait()
        pl.semaphore_wait(bar, len(peers))

    started = []

    def remote(src, dst, ssem, rsem, dev):
        return pltpu.make_async_remote_copy(
            src_ref=src, dst_ref=dst, send_sem=ssem, recv_sem=rsem, device_id=dev,
            device_id_type=pl.DeviceIdType.MESH,
        )

    def go(*a):
        c = remote(*a)
        c.start()
        started.append(c)

    def ag_start(c):
        s, h = c // 2, c % 2
        for v, (dev, here, there) in enumerate(
            ((up, below(s), below(s + 1)), (down, above(s), above(s + 1)))
        ):
            part_rows = pl.ds(half * (h if v == 0 else 1 - h), half)
            go(panels.at[here, part_rows], panels.at[there, part_rows], ag_s.at[v, c], ag_r.at[v, c], dev)

    def ag_step(c):
        s, h = c // 2, c % 2
        with scope(f"panel_hop_{c}"):
            for v, (dev, there) in enumerate(((up, below(s + 1)), (down, above(s + 1)))):
                ref = panels.at[there, pl.ds(half * (h if v == 0 else 1 - h), half)]
                remote(ref, ref, ag_s.at[v, c], ag_r.at[v, c], dev).wait_recv()
            if c + 2 < CHUNKS:
                ag_start(c + 2)

    ag_start(0)
    ag_start(1)

    def iota(shape, d):
        return lax.broadcasted_iota(jnp.int32, shape, d)

    def hot(cond):
        return jnp.where(cond, 1.0, 0.0)

    with scope("routing"):
        for c in routes_in:
            c.wait()
        n_panels = panel_ref.shape[1]
        owners = NY * NZ
        rank = 64
        named = hot(iota((n_panels, rows), 0) == ids_ref[...]).astype(BF16)
        mapped = hot(iota((n_panels, n_panels), 0) == panel_ref[...]).astype(BF16)
        panel_hot = dot(mapped, named, 1, 0)
        panel = jnp.sum(panel_hot * iota((n_panels, rows), 0).astype(F32), axis=0, keepdims=True).astype(jnp.int32)
        owner = panel // 2
        within = panel - owner * 2
        own_y = owner // NZ
        away = owner - own_y * NZ - zi
        away = jnp.where(away < 0, away + NZ, away)
        order = jnp.where(away == FAR, NZ - 1, jnp.where(away < FAR, 2 * away, 2 * (NZ - away) - 1))
        block = own_y * NZ + order
        block_hot = hot(iota((owners, rows), 0) == block)
        before = hot(iota((rows, rows), 0) < iota((rows, rows), 1)).astype(BF16)
        counts = dot(block_hot.astype(BF16), before, 1, 0) * block_hot
        earlier = jnp.sum(counts, axis=0, keepdims=True).astype(jnp.int32)
        slot = block * PAD + earlier
        which = jnp.max(block_hot * within.astype(F32), axis=1, keepdims=True)
        pick = hot((iota((owners, 128), 1) // rank).astype(F32) == which)
        last = iota((NZ * PAD, 128), 0) % PAD == PAD - 1
        tok_in.wait()
    def rows_out(q):
        place = hot(iota((NZ * PAD, rows), 0) + q * NZ * PAD == slot).astype(BF16)
        t = dot(place, tok[...], 1, 0).astype(BF16)
        u = dot(place, up_ref[...], 1, 0)
        marks = jnp.broadcast_to(pick[q * NZ : (q + 1) * NZ].reshape(NZ, 1, 128), (NZ, PAD, 128))
        u = jnp.where(last, marks.reshape(NZ * PAD, 128), u).astype(BF16)
        send[q, :, :, :feats] = t.reshape(NZ, PAD, feats)
        send[q, :, :, feats:] = u.reshape(NZ, PAD, 128)

    with scope("rows_placed"):
        rows_out(0)
        rows_out(1)
    ag_step(0)
    with scope("rows_out"):
        rows_out(2)
        rows_out(3)
        mine_rows = pl.ds(pl.multiple_of(yi * PAD, PAD), PAD)
        for d in range(1, NY):
            go(send.at[lax.rem(yi + d, NY)], rbuf.at[:, mine_rows, :], y_s.at[d], y_r.at[d], y_peer(d))
        own = pltpu.make_async_copy(send.at[yi], rbuf.at[:, mine_rows, :], loc.at[0])
        own.start()
    with scope("cotangents_out"):
        for d in range(1, NM):
            go(up_ref, ua.at[:, lanes(m)], u_s.at[d], u_r.at[d], m_peer(d))
        ua[:, lanes(m)] = up_ref[...]
    ag_step(1)

    def base(j):
        r = dot(tok[...], w[:, 256 * j : 256 * j + 256], 1, 0)
        fs[2 * j] = r[:, :128]
        fs[2 * j + 1] = r[:, 128:]

    with scope("base"):
        w_in.wait()
        base(0)
        base(1)
    ag_step(2)
    with scope("base_more"):
        base(2)
        base(3)
    ag_step(3)
    with scope("row_places"):
        ones = jnp.ones((owners, 128), BF16)
        blocks = dot((block_hot * iota((owners, rows), 0).astype(F32)).astype(BF16), ones, 0, 0)
        slot_col = blocks * PAD + dot(counts.astype(BF16), ones, 0, 0)

    def row_places(j):
        back_place[:, 128 * j : 128 * j + 128] = hot(
            (iota((rows, 128), 1) + 128 * j).astype(F32) == slot_col
        ).astype(BF16)

    for j in range(4):
        row_places(j)
    ag_step(4)
    for j in range(4, 8):
        row_places(j)
    with scope("cotangents_wait"):
        for d in range(1, NM):
            ref = ua.at[:, lanes(lax.rem(m + NM - d, NM))]
            remote(ref, ref, u_s.at[d], u_r.at[d], m_peer(d)).wait_recv()
    for c in range(4):
        ag_step(5 + c)
        with scope("base_gradient"):
            r = pl.ds(256 * c, 256)
            fg[:, r] = dot(ua[...], w[r, :], 1, 1)
    ag_step(9)

    lane = iota((NY * PAD, 128), 1) < 64

    def masks_of(v):
        n = v.shape[0] // PAD
        v = v.astype(F32).reshape(n, PAD, 128)[:, PAD - 1 :, :]
        return jnp.broadcast_to(v, (n, PAD, 128)).reshape(n * PAD, 128)

    def masks(k):
        return masks_of(rbuf[k, :, feats:])

    def rows_wait():
        with scope("rows_wait"):
            own.wait()
            for d in range(1, NY):
                ref = rbuf.at[:, pl.ds(pl.multiple_of(lax.rem(yi + NY - d, NY) * PAD, PAD), PAD), :]
                remote(ref, ref, y_s.at[d], y_r.at[d], y_peer(d)).wait_recv()

    def first(k):
        mask = masks(k)
        inner = dot(rbuf[k, :, :feats], panels[k, :, :feats], 1, 1) * mask
        back = dot(rbuf[k, :, feats:], panels[k, :, feats:], 1, 1) * mask
        inner = inner + pltpu.roll(inner, 64, 1)
        back = back + pltpu.roll(back, 64, 1)
        pk[k] = jnp.where(lane, inner, back)

    def x_send(b):
        k0, k1 = BATCHES[b]
        for d in range(1, NM):
            p = lax.rem(m + d, NM)
            go(pk.at[k0:k1, pl.ds(pl.multiple_of(p * 8, 8), 8), :], rsr.at[m, k0:k1],
               xs_s.at[b, d], xs_r.at[b, d], m_peer(d))

    def x_reduce(b):
        k0, k1 = BATCHES[b]
        mine = pl.ds(pl.multiple_of(m * 8, 8), 8)
        acc = pk[k0:k1, mine, :]
        for d in range(1, NM):
            src = lax.rem(m + NM - d, NM)
            ref = rsr.at[src, k0:k1]
            remote(ref, ref, xs_s.at[b, d], xs_r.at[b, d], m_peer(d)).wait_recv()
            acc = acc + rsr[src, k0:k1]
        pkf[k0:k1, mine, :] = acc.astype(BF16).astype(F32)
        for d in range(1, NM):
            ref = pkf.at[k0:k1, mine, :]
            go(ref, ref, xg_s.at[b, d], xg_r.at[b, d], m_peer(d))

    def x_finish(b):
        k0, k1 = BATCHES[b]
        for d in range(1, NM):
            src = lax.rem(m + NM - d, NM)
            ref = pkf.at[k0:k1, pl.ds(pl.multiple_of(src * 8, 8), 8), :]
            remote(ref, ref, xg_s.at[b, d], xg_r.at[b, d], m_peer(d)).wait_recv()

    def spread_of(v, mask):
        left = iota(v.shape, 1) < 64
        r = pltpu.roll(v, 64, 1)
        return (jnp.where(left, v, r) * mask).astype(BF16), (jnp.where(left, r, v) * mask).astype(BF16)

    def spread(k):
        return spread_of(pkf[k], masks(k))

    def sums(k):
        inner, back = spread(k)
        part[k, :, :feats] = dot(back, rbuf[k, :, :feats], 0, 0)
        part[k, :, feats:] = dot(inner, rbuf[k, :, feats:], 0, 0)

    def rows_back(k):
        inner, back = spread(k)
        grad = (SCALE * dot(back, panels[k, :, :feats], 1, 0)).astype(BF16)
        delta = (SCALE * dot(inner, panels[k, :, feats:], 1, 0)).astype(BF16)
        for q in range(NY):
            rets[q, k, :, :feats] = grad[q * PAD : (q + 1) * PAD]
            rets[q, k, :, feats:] = delta[q * PAD : (q + 1) * PAD]

    def whole_send(i, j0, j1):
        for j in range(j0, j1):
            short[j] = pk[13 + j].astype(BF16)
            whole[m, j] = short[j]
        for d in range(1, NM):
            go(short.at[j0:j1], whole.at[m, j0:j1], b_s.at[i, d], b_r.at[i, d], m_peer(d))

    def whole_finish(i, j0, j1):
        for d in range(1, NM):
            ref = whole.at[lax.rem(m + NM - d, NM), j0:j1]
            remote(ref, ref, b_s.at[i, d], b_r.at[i, d], m_peer(d)).wait_recv()
        for j in range(j0, j1):
            total = sum(whole[p, j].astype(F32) for p in range(NM))
            pkf[13 + j] = total.astype(BF16).astype(F32)

    near = NY * PAD
    far = near // 2
    far_pieces = (
        (0, up, 14, pl.ds(0, near), pl.ds(0, near)),
        (0, down, 13, pl.ds(0, near), pl.ds(0, near)),
        (1, up2, 15, pl.ds(0, far), pl.ds(near, far)),
        (1, down2, 15, pl.ds(far, far), pl.ds(near, far)),
    )

    def far_rows_send():
        for i, (_, dev, k, src, dst) in enumerate(far_pieces):
            go(rbuf.at[k, src], far_rows.at[i % 2, dst], fr_s.at[i], fr_r.at[i], dev)

    def far_ranks_send(stage):
        for i, (at_stage, dev, k, src, dst) in enumerate(far_pieces):
            if at_stage == stage:
                go(pkf.at[k, src], far_ranks.at[i % 2, dst], fk_s.at[i], fk_r.at[i], dev)

    def far_sums():
        for i, (_, dev, k, src, dst) in enumerate(far_pieces):
            rows_ref, ranks_ref = far_rows.at[i % 2, dst], far_ranks.at[i % 2, dst]
            remote(rows_ref, rows_ref, fr_s.at[i], fr_r.at[i], dev).wait_recv()
            remote(ranks_ref, ranks_ref, fk_s.at[i], fk_r.at[i], dev).wait_recv()
        for v, k in enumerate((12, 11)):
            inner, back = spread_of(far_ranks[v], masks_of(far_rows[v, :, feats:]))
            part[k, :, :feats] += dot(back, far_rows[v, :, :feats], 0, 0)
            part[k, :, feats:] += dot(inner, far_rows[v, :, feats:], 0, 0)

    locals_ = [own]

    def ret_send(i, k0, k1):
        for d in range(1, NY):
            go(rets.at[lax.rem(yi + d, NY), k0:k1], ret.at[yi, k0:k1], rt_s.at[i, d], rt_r.at[i, d], y_peer(d))
        c = pltpu.make_async_copy(rets.at[yi, k0:k1], ret.at[yi, k0:k1], loc.at[1 + i])
        c.start()
        locals_.append(c)

    def ret_wait(i, k0, k1):
        locals_[1 + i].wait()
        for d in range(1, NY):
            ref = ret.at[lax.rem(yi + NY - d, NY), k0:k1]
            remote(ref, ref, rt_s.at[i, d], rt_r.at[i, d], y_peer(d)).wait_recv()

    rows_wait()
    with scope("ranks_0"):
        for k in (9, 10, 7, 8):
            first(k)
    ag_step(10)
    with scope("ranks_1"):
        for k in (5, 6, 3):
            first(k)
    ag_step(11)
    with scope("ranks_2"):
        first(11)
        first(12)
        x_send(1)
        first(4)
    ag_step(12)
    with scope("ranks_3"):
        for k in range(3):
            first(k)
        x_send(0)
        x_reduce(1)
    ag_step(13)
    with scope("ranks_4"):
        first(13)
        first(14)
        whole_send(0, 0, 2)
        x_finish(1)
        sums(12)
        sums(11)
    ag_step(14)
    with scope("far_rows_out"):
        far_rows_send()
    with scope("ranks_5"):
        first(15)
        whole_send(1, 2, 3)
    with scope("whole_0"):
        whole_finish(0, 0, 2)
        far_ranks_send(0)
        x_reduce(0)
    with scope("whole_1"):
        whole_finish(1, 2, 3)
        far_ranks_send(1)
    with scope("finish_0"):
        sums(10)
        sums(9)
        x_finish(0)
        rows_back(0)
    with scope("far_sums"):
        far_sums()

    def piece(v, c):
        s, h = SUM_HOPS - c // 2, c % 2
        return (above(s) if v == 0 else below(s)), pl.ds(half * (h if v == 0 else 1 - h), half)

    def rs_step(c):
        with scope(f"sum_hop_{c}"):
            for v, dev in enumerate((up, down)):
                k, part_rows = piece(v, c)
                x = part[k, part_rows, :]
                if c >= 2:
                    ref = prec.at[v, c - 2]
                    remote(ref, ref, rs_s.at[v, c - 2], rs_r.at[v, c - 2], dev).wait_recv()
                    x = x + prec[v, c - 2].astype(F32)
                psend[v, c] = x.astype(BF16)
                go(psend.at[v, c], prec.at[v, c], rs_s.at[v, c], rs_r.at[v, c], dev)

    rs_step(0)
    rs_step(1)
    with scope("base_out"):
        for d in range(1, NM):
            p = lax.rem(m + d, NM)
            go(fs.at[p], fr.at[m], f_s.at[d], f_r.at[d], m_peer(d))
    for i, s in enumerate(range(SUM_HOPS - 1, 0, -1)):
        with scope("sums"):
            if i:
                sums(2 * s)
                sums(2 * s - 1)
        rs_step(2 + 2 * i)
        if i == 0:
            with scope("rows_back_b"):
                for k in range(1, 5):
                    rows_back(k)
        if i == 1:
            with scope("rows_back_c"):
                for k in range(5, 8):
                    rows_back(k)
                ret_send(0, 0, 8)
        if i == 2:
            with scope("rows_back_d"):
                for k in range(10, 13):
                    rows_back(k)
        if i == 4:
            with scope("base_wait"):
                acc = fs[m]
                for d in range(1, NM):
                    src = lax.rem(m + NM - d, NM)
                    remote(fr.at[src], fr.at[src], f_s.at[d], f_r.at[d], m_peer(d)).wait_recv()
                    acc = acc + fr[src]
                fs[m] = acc
        rs_step(3 + 2 * i)
        if i in (0, 1):
            with scope("rows_back_e"):
                rows_back(8 + i)
        if i == 2:
            with scope("rows_back_f"):
                for k in range(13, 16):
                    rows_back(k)
                ret_send(1, 8, 16)
    sums(0)
    with scope("returned_wait"):
        ret_wait(0, 0, 8)
        ret_wait(1, 8, 16)
    with scope("outputs"):
        mine = ret[...].reshape(NY * NZ * PAD, wide)
        for j in range(4):
            r = pl.ds(128 * j, 128)
            place = back_place[r]
            ua[r] = (fg[r] + dot(place, mine[:, :feats], 1, 0)).astype(BF16)
            proj[r] = (fs[m, r] + dot(place, mine[:, feats:], 1, 0)).astype(BF16)
        tig_out = pltpu.make_async_copy(ua, tig_ref, loc.at[5])
        proj_out = pltpu.make_async_copy(proj, proj_ref, loc.at[6])
        tig_out.start()
        proj_out.start()
    with scope("last_sums"):
        for v, dev in enumerate((up, down)):
            for c in (SUMS - 2, SUMS - 1):
                ref = prec.at[v, c]
                remote(ref, ref, rs_s.at[v, c], rs_r.at[v, c], dev).wait_recv()
        for p in range(2):
            scale = SCALE * (1 - flags_ref[p]).astype(F32)
            c0, c1 = (SUMS - 2, SUMS - 1) if p == 0 else (SUMS - 1, SUMS - 2)
            r = slice(p * half, (p + 1) * half)
            v = scale * (part[0, r] + prec[0, c0].astype(F32) + prec[1, c1].astype(F32))
            down_ref[r] = v[:, :feats].astype(BF16)
            upg_ref[r] = v[:, feats:].astype(BF16)
    with scope("sent"):
        tig_out.wait()
        proj_out.wait()
        for c in started:
            c.wait_send()


def fused(tokens, weight, at, b, ids, panel_of, flags, upstream):
    rows, feats = tokens.shape
    n = at.shape[0]
    half = n // 2
    wide = feats + 128
    vm = pl.BlockSpec(memory_space=pltpu.VMEM)
    hbm = pl.BlockSpec(memory_space=pl.ANY)
    dma = pltpu.SemaphoreType.DMA
    group = NY * PAD
    nb = len(BATCHES)
    return pl.pallas_call(
        kernel,
        out_shape=(
            jax.ShapeDtypeStruct((rows, 128), BF16),
            jax.ShapeDtypeStruct((rows, feats), BF16),
            jax.ShapeDtypeStruct((n, feats), BF16),
            jax.ShapeDtypeStruct((n, 128), BF16),
        ),
        in_specs=[hbm, hbm, hbm, hbm, hbm, hbm, pl.BlockSpec(memory_space=pltpu.SMEM), hbm],
        out_specs=(hbm, hbm, vm, vm),
        scratch_shapes=[
            pltpu.VMEM((rows, feats), BF16),
            pltpu.VMEM(weight.shape, BF16),
            pltpu.VMEM(ids.shape, jnp.int32),
            pltpu.VMEM(panel_of.shape, jnp.int32),
            pltpu.VMEM(upstream.shape, BF16),
            pltpu.VMEM((rows, NM * 128), BF16),
            pltpu.VMEM((NM, rows, 128), F32),
            pltpu.VMEM((NM, rows, 128), F32),
            pltpu.VMEM((rows, feats), F32),
            pltpu.VMEM((rows, NY * NZ * PAD), BF16),
            pltpu.VMEM((NY, NZ, PAD, wide), BF16),
            pltpu.VMEM((NY, NZ, PAD, wide), BF16),
            pltpu.VMEM((NZ, n, wide), BF16),
            pltpu.VMEM((NZ, group, wide), BF16),
            pltpu.VMEM((NY, NZ, PAD, wide), BF16),
            pltpu.VMEM((NZ, group, 128), F32),
            pltpu.VMEM((NM, NZ, group // NM, 128), F32),
            pltpu.VMEM((NZ, group, 128), F32),
            pltpu.VMEM((3, group, 128), BF16),
            pltpu.VMEM((NM, 3, group, 128), BF16),
            pltpu.VMEM((2, group + group // 2, wide), BF16),
            pltpu.VMEM((2, group + group // 2, 128), F32),
            pltpu.VMEM((rows, 128), BF16),
            pltpu.VMEM((NZ, n, wide), F32),
            pltpu.VMEM((2, SUMS, half, wide), BF16),
            pltpu.VMEM((2, SUMS, half, wide), BF16),
            dma((2, CHUNKS)), dma((2, CHUNKS)),
            dma((NY,)), dma((NY,)),
            dma((2, NY)), dma((2, NY)),
            dma((nb, NM)), dma((nb, NM)),
            dma((nb, NM)), dma((nb, NM)),
            dma((2, SUMS)), dma((2, SUMS)),
            dma((NM,)), dma((NM,)),
            dma((NM,)), dma((NM,)),
            dma((2, NM)), dma((2, NM)),
            dma((4,)), dma((4,)),
            dma((4,)), dma((4,)),
            dma((12,)),
        ],
        compiler_params=pltpu.CompilerParams(
            collective_id=0, has_side_effects=True, vmem_limit_bytes=58 * 2**20
        ),
        cost_estimate=pl.CostEstimate(flops=5 * 10**9, bytes_accessed=10**7, transcendentals=0),
    )(tokens, weight, at, b, ids, panel_of, flags, upstream)


def copies(*refs):
    n = (len(refs) - 2) // 3
    ins, outs, bufs, (in_sems, out_sems) = refs[:n], refs[n : 2 * n], refs[2 * n : 3 * n], refs[3 * n :]
    parts = []
    for i in range(n):
        cuts = 4 if ins[i].shape[0] * ins[i].shape[1] > 2**18 else 1
        step = ins[i].shape[0] // cuts
        for j in range(cuts):
            r = pl.ds(step * j, step)
            k = len(parts)
            parts.append((
                pltpu.make_async_copy(ins[i].at[r], bufs[i].at[r], in_sems.at[k]),
                pltpu.make_async_copy(bufs[i].at[r], outs[i].at[r], out_sems.at[k]),
            ))
    for c, _ in parts:
        c.start()
    for c, d in parts:
        c.wait()
        d.start()
    for _, d in parts:
        d.wait()


def settle(arrays):
    hbm = pl.BlockSpec(memory_space=pl.ANY)
    dma = pltpu.SemaphoreType.DMA
    return pl.pallas_call(
        copies,
        out_shape=tuple(jax.ShapeDtypeStruct(a.shape, a.dtype) for a in arrays),
        in_specs=[hbm] * len(arrays),
        out_specs=(hbm,) * len(arrays),
        scratch_shapes=[pltpu.VMEM(a.shape, a.dtype) for a in arrays]
        + [dma((4 * len(arrays),)), dma((4 * len(arrays),))],
    )(*arrays)


def shards(tokens, base_weight, adapter_a, adapter_b, row_ids, panel_of, stop_flags, upstream):
    per_owner, feats, rank = adapter_a.shape
    vals = upstream.shape[1]
    at = jnp.transpose(adapter_a, (0, 2, 1)).reshape(per_owner * rank, feats)
    b = adapter_b.reshape(per_owner * rank, vals)
    projected, gradient, down, up = settle(fused(
        tokens, base_weight, at, b, row_ids.reshape(1, -1), panel_of.reshape(1, -1), stop_flags, upstream
    ))
    return (
        projected,
        gradient,
        jnp.transpose(down.reshape(per_owner, rank, feats), (0, 2, 1)),
        up.reshape(per_owner, rank, vals),
    )


def solution(mesh):
    fine = Mesh(mesh.devices.reshape(NY, NZ, NX, NC), ("y", "z", "x", "core"))
    placed = (
        P(DP, MP),
        P(MP, None),
        P(DP, MP, None),
        P(DP, None, MP),
        P(DP),
        P(),
        P(DP),
        P(DP, MP),
    )
    return jax.shard_map(
        shards,
        mesh=fine,
        in_specs=placed,
        out_specs=(P(DP, MP), P(DP, MP), P(DP, MP, None), P(DP, None, MP)),
        check_vma=False,
    )
```

```python
import jax
import jax.numpy as jnp
from jax import lax
from jax.experimental import pallas as pl
from jax.experimental.pallas import tpu as pltpu
from jax.sharding import Mesh
from jax.sharding import PartitionSpec as P

SCALE = 2.0
F32 = jnp.float32
BF16 = jnp.bfloat16
NY, NZ, NX, NC = 4, 16, 4, 2
NM = NX * NC
PAD = 16
FAR = NZ // 2
DP = ("y", "z")
MP = ("x", "core")
BATCHES = ((0, 9), (9, 13))
CHUNKS = 2 * FAR - 1
SUM_HOPS = FAR - 2
SUMS = 2 * SUM_HOPS


def dot(a, b, ca, cb):
    return lax.dot_general(a, b, (((ca,), (cb,)), ((), ())), preferred_element_type=F32)


def below(s):
    return 0 if s == 0 else (NZ - 1 if s == FAR else 2 * s - 1)


def above(s):
    return 0 if s == 0 else (NZ - 1 if s == FAR else 2 * s)


def kernel(tok_hbm, w_hbm, at_hbm, b_hbm, ids_hbm, panel_hbm, flags_ref, up_hbm,
           proj_ref, tig_ref, down_ref, upg_ref,
           tok, w, ids_ref, panel_ref, up_ref, ua, fs, fr, fg, back_place, send, ret, panels, rbuf, rets, pk, rsr, pkf, short, whole, far_rows, far_ranks, proj, part, psend, prec,
           ag_s, ag_r, y_s, y_r, rt_s, rt_r, xs_s, xs_r, xg_s, xg_r, rs_s, rs_r, u_s, u_r, f_s, f_r, b_s, b_r, fr_s, fr_r, fk_s, fk_r, loc):
    scope = jax.named_scope
    rows, feats = tok.shape
    wide = feats + 128
    half = at_hbm.shape[0] // 2
    yi, zi, xi, ci = (lax.axis_index(n) for n in ("y", "z", "x", "core"))
    m = xi * NC + ci
    up = {"z": lax.rem(zi + 1, NZ)}
    down = {"z": lax.rem(zi + NZ - 1, NZ)}
    up2 = {"z": lax.rem(zi + 2, NZ)}
    down2 = {"z": lax.rem(zi + NZ - 2, NZ)}

    def y_peer(d):
        return {"y": lax.rem(yi + d, NY)}

    def m_peer(d):
        p = lax.rem(m + d, NM)
        return {"x": p // NC, "core": lax.rem(p, NC)}

    def lanes(p):
        return pl.ds(pl.multiple_of(p * 128, 128), 128)

    def load(src, dst, i):
        c = pltpu.make_async_copy(src, dst, loc.at[i])
        c.start()
        return c

    with scope("entry"):
        bar = pltpu.get_barrier_semaphore()
        peers = [up, down, up2, down2] + [y_peer(d) for d in range(1, NY)] + [m_peer(d) for d in range(1, NM)]
        for p in peers:
            pl.semaphore_signal(bar, inc=1, device_id=p, device_id_type=pl.DeviceIdType.MESH)
        panels_in = [
            load(at_hbm, panels.at[0, :, pl.ds(0, feats)], 7),
            load(b_hbm, panels.at[0, :, pl.ds(feats, 128)], 8),
        ]
        routes_in = [load(ids_hbm, ids_ref, 9), load(panel_hbm, panel_ref, 10), load(up_hbm, up_ref, 11)]
        tok_in = load(tok_hbm, tok, 3)
        w_in = load(w_hbm, w, 4)
        for c in panels_in:
            c.wait()
        pl.semaphore_wait(bar, len(peers))

    started = []

    def remote(src, dst, ssem, rsem, dev):
        return pltpu.make_async_remote_copy(
            src_ref=src, dst_ref=dst, send_sem=ssem, recv_sem=rsem, device_id=dev,
            device_id_type=pl.DeviceIdType.MESH,
        )

    def go(*a):
        c = remote(*a)
        c.start()
        started.append(c)

    def ag_start(c):
        s, h = c // 2, c % 2
        for v, (dev, here, there) in enumerate(
            ((up, below(s), below(s + 1)), (down, above(s), above(s + 1)))
        ):
            part_rows = pl.ds(half * (h if v == 0 else 1 - h), half)
            go(panels.at[here, part_rows], panels.at[there, part_rows], ag_s.at[v, c], ag_r.at[v, c], dev)

    def ag_step(c):
        s, h = c // 2, c % 2
        with scope(f"panel_hop_{c}"):
            for v, (dev, there) in enumerate(((up, below(s + 1)), (down, above(s + 1)))):
                ref = panels.at[there, pl.ds(half * (h if v == 0 else 1 - h), half)]
                remote(ref, ref, ag_s.at[v, c], ag_r.at[v, c], dev).wait_recv()
            if c + 2 < CHUNKS:
                ag_start(c + 2)

    ag_start(0)
    ag_start(1)

    def iota(shape, d):
        return lax.broadcasted_iota(jnp.int32, shape, d)

    def hot(cond):
        return jnp.where(cond, 1.0, 0.0)

    with scope("routing"):
        for c in routes_in:
            c.wait()
        n_panels = panel_ref.shape[1]
        owners = NY * NZ
        rank = 64
        named = hot(iota((n_panels, rows), 0) == ids_ref[...]).astype(BF16)
        mapped = hot(iota((n_panels, n_panels), 0) == panel_ref[...]).astype(BF16)
        panel_hot = dot(mapped, named, 1, 0)
        panel = jnp.sum(panel_hot * iota((n_panels, rows), 0).astype(F32), axis=0, keepdims=True).astype(jnp.int32)
        owner = panel // 2
        within = panel - owner * 2
        own_y = owner // NZ
        away = owner - own_y * NZ - zi
        away = jnp.where(away < 0, away + NZ, away)
        order = jnp.where(away == FAR, NZ - 1, jnp.where(away < FAR, 2 * away, 2 * (NZ - away) - 1))
        block = own_y * NZ + order
        block_hot = hot(iota((owners, rows), 0) == block)
        before = hot(iota((rows, rows), 0) < iota((rows, rows), 1)).astype(BF16)
        counts = dot(block_hot.astype(BF16), before, 1, 0) * block_hot
        earlier = jnp.sum(counts, axis=0, keepdims=True).astype(jnp.int32)
        slot = block * PAD + earlier
        which = jnp.max(block_hot * within.astype(F32), axis=1, keepdims=True)
        pick = hot((iota((owners, 128), 1) // rank).astype(F32) == which)
        last = iota((NZ * PAD, 128), 0) % PAD == PAD - 1
        tok_in.wait()
    def rows_out(q):
        place = hot(iota((NZ * PAD, rows), 0) + q * NZ * PAD == slot).astype(BF16)
        t = dot(place, tok[...], 1, 0).astype(BF16)
        u = dot(place, up_ref[...], 1, 0)
        marks = jnp.broadcast_to(pick[q * NZ : (q + 1) * NZ].reshape(NZ, 1, 128), (NZ, PAD, 128))
        u = jnp.where(last, marks.reshape(NZ * PAD, 128), u).astype(BF16)
        send[q, :, :, :feats] = t.reshape(NZ, PAD, feats)
        send[q, :, :, feats:] = u.reshape(NZ, PAD, 128)

    with scope("rows_placed"):
        rows_out(0)
        rows_out(1)
    ag_step(0)
    with scope("rows_out"):
        rows_out(2)
        rows_out(3)
        mine_rows = pl.ds(pl.multiple_of(yi * PAD, PAD), PAD)
        for d in range(1, NY):
            go(send.at[lax.rem(yi + d, NY)], rbuf.at[:, mine_rows, :], y_s.at[d], y_r.at[d], y_peer(d))
        own = pltpu.make_async_copy(send.at[yi], rbuf.at[:, mine_rows, :], loc.at[0])
        own.start()
    with scope("cotangents_out"):
        for d in range(1, NM):
            go(up_ref, ua.at[:, lanes(m)], u_s.at[d], u_r.at[d], m_peer(d))
        ua[:, lanes(m)] = up_ref[...]
    ag_step(1)

    def base(j):
        r = dot(tok[...], w[:, 256 * j : 256 * j + 256], 1, 0)
        fs[2 * j] = r[:, :128]
        fs[2 * j + 1] = r[:, 128:]

    with scope("base"):
        w_in.wait()
        base(0)
        base(1)
    ag_step(2)
    with scope("base_more"):
        base(2)
        base(3)
    ag_step(3)
    with scope("row_places"):
        ones = jnp.ones((owners, 128), BF16)
        blocks = dot((block_hot * iota((owners, rows), 0).astype(F32)).astype(BF16), ones, 0, 0)
        slot_col = blocks * PAD + dot(counts.astype(BF16), ones, 0, 0)

    def row_places(j):
        back_place[:, 128 * j : 128 * j + 128] = hot(
            (iota((rows, 128), 1) + 128 * j).astype(F32) == slot_col
        ).astype(BF16)

    for j in range(4):
        row_places(j)
    ag_step(4)
    for j in range(4, 8):
        row_places(j)
    with scope("cotangents_wait"):
        for d in range(1, NM):
            ref = ua.at[:, lanes(lax.rem(m + NM - d, NM))]
            remote(ref, ref, u_s.at[d], u_r.at[d], m_peer(d)).wait_recv()
    for c in range(4):
        ag_step(5 + c)
        with scope("base_gradient"):
            r = pl.ds(256 * c, 256)
            fg[:, r] = dot(ua[...], w[r, :], 1, 1)
    ag_step(9)

    lane = iota((NY * PAD, 128), 1) < 64

    def masks_of(v):
        n = v.shape[0] // PAD
        v = v.astype(F32).reshape(n, PAD, 128)[:, PAD - 1 :, :]
        return jnp.broadcast_to(v, (n, PAD, 128)).reshape(n * PAD, 128)

    def masks(k):
        return masks_of(rbuf[k, :, feats:])

    def rows_wait():
        with scope("rows_wait"):
            own.wait()
            for d in range(1, NY):
                ref = rbuf.at[:, pl.ds(pl.multiple_of(lax.rem(yi + NY - d, NY) * PAD, PAD), PAD), :]
                remote(ref, ref, y_s.at[d], y_r.at[d], y_peer(d)).wait_recv()

    def first(k):
        mask = masks(k)
        inner = dot(rbuf[k, :, :feats], panels[k, :, :feats], 1, 1) * mask
        back = dot(rbuf[k, :, feats:], panels[k, :, feats:], 1, 1) * mask
        inner = inner + pltpu.roll(inner, 64, 1)
        back = back + pltpu.roll(back, 64, 1)
        pk[k] = jnp.where(lane, inner, back)

    def x_send(b):
        k0, k1 = BATCHES[b]
        for d in range(1, NM):
            p = lax.rem(m + d, NM)
            go(pk.at[k0:k1, pl.ds(pl.multiple_of(p * 8, 8), 8), :], rsr.at[m, k0:k1],
               xs_s.at[b, d], xs_r.at[b, d], m_peer(d))

    def x_reduce(b):
        k0, k1 = BATCHES[b]
        mine = pl.ds(pl.multiple_of(m * 8, 8), 8)
        acc = pk[k0:k1, mine, :]
        for d in range(1, NM):
            src = lax.rem(m + NM - d, NM)
            ref = rsr.at[src, k0:k1]
            remote(ref, ref, xs_s.at[b, d], xs_r.at[b, d], m_peer(d)).wait_recv()
            acc = acc + rsr[src, k0:k1]
        pkf[k0:k1, mine, :] = acc.astype(BF16).astype(F32)
        for d in range(1, NM):
            ref = pkf.at[k0:k1, mine, :]
            go(ref, ref, xg_s.at[b, d], xg_r.at[b, d], m_peer(d))

    def x_finish(b):
        k0, k1 = BATCHES[b]
        for d in range(1, NM):
            src = lax.rem(m + NM - d, NM)
            ref = pkf.at[k0:k1, pl.ds(pl.multiple_of(src * 8, 8), 8), :]
            remote(ref, ref, xg_s.at[b, d], xg_r.at[b, d], m_peer(d)).wait_recv()

    def spread_of(v, mask):
        left = iota(v.shape, 1) < 64
        r = pltpu.roll(v, 64, 1)
        return (jnp.where(left, v, r) * mask).astype(BF16), (jnp.where(left, r, v) * mask).astype(BF16)

    def spread(k):
        return spread_of(pkf[k], masks(k))

    def sums(k):
        inner, back = spread(k)
        part[k, :, :feats] = dot(back, rbuf[k, :, :feats], 0, 0)
        part[k, :, feats:] = dot(inner, rbuf[k, :, feats:], 0, 0)

    def rows_back(k):
        inner, back = spread(k)
        grad = (SCALE * dot(back, panels[k, :, :feats], 1, 0)).astype(BF16)
        delta = (SCALE * dot(inner, panels[k, :, feats:], 1, 0)).astype(BF16)
        for q in range(NY):
            rets[q, k, :, :feats] = grad[q * PAD : (q + 1) * PAD]
            rets[q, k, :, feats:] = delta[q * PAD : (q + 1) * PAD]

    def whole_send(i, j0, j1):
        for j in range(j0, j1):
            short[j] = pk[13 + j].astype(BF16)
            whole[m, j] = short[j]
        for d in range(1, NM):
            go(short.at[j0:j1], whole.at[m, j0:j1], b_s.at[i, d], b_r.at[i, d], m_peer(d))

    def whole_finish(i, j0, j1):
        for d in range(1, NM):
            ref = whole.at[lax.rem(m + NM - d, NM), j0:j1]
            remote(ref, ref, b_s.at[i, d], b_r.at[i, d], m_peer(d)).wait_recv()
        for j in range(j0, j1):
            total = sum(whole[p, j].astype(F32) for p in range(NM))
            pkf[13 + j] = total.astype(BF16).astype(F32)

    near = NY * PAD
    far = near // 2
    far_pieces = (
        (0, up, 14, pl.ds(0, near), pl.ds(0, near)),
        (0, down, 13, pl.ds(0, near), pl.ds(0, near)),
        (1, up2, 15, pl.ds(0, far), pl.ds(near, far)),
        (1, down2, 15, pl.ds(far, far), pl.ds(near, far)),
    )

    def far_rows_send():
        for i, (_, dev, k, src, dst) in enumerate(far_pieces):
            go(rbuf.at[k, src], far_rows.at[i % 2, dst], fr_s.at[i], fr_r.at[i], dev)

    def far_ranks_send(stage):
        for i, (at_stage, dev, k, src, dst) in enumerate(far_pieces):
            if at_stage == stage:
                go(pkf.at[k, src], far_ranks.at[i % 2, dst], fk_s.at[i], fk_r.at[i], dev)

    def far_sums():
        for i, (_, dev, k, src, dst) in enumerate(far_pieces):
            rows_ref, ranks_ref = far_rows.at[i % 2, dst], far_ranks.at[i % 2, dst]
            remote(rows_ref, rows_ref, fr_s.at[i], fr_r.at[i], dev).wait_recv()
            remote(ranks_ref, ranks_ref, fk_s.at[i], fk_r.at[i], dev).wait_recv()
        for v, k in enumerate((12, 11)):
            inner, back = spread_of(far_ranks[v], masks_of(far_rows[v, :, feats:]))
            part[k, :, :feats] += dot(back, far_rows[v, :, :feats], 0, 0)
            part[k, :, feats:] += dot(inner, far_rows[v, :, feats:], 0, 0)

    locals_ = [own]

    def ret_send(i, k0, k1):
        for d in range(1, NY):
            go(rets.at[lax.rem(yi + d, NY), k0:k1], ret.at[yi, k0:k1], rt_s.at[i, d], rt_r.at[i, d], y_peer(d))
        c = pltpu.make_async_copy(rets.at[yi, k0:k1], ret.at[yi, k0:k1], loc.at[1 + i])
        c.start()
        locals_.append(c)

    def ret_wait(i, k0, k1):
        locals_[1 + i].wait()
        for d in range(1, NY):
            ref = ret.at[lax.rem(yi + NY - d, NY), k0:k1]
            remote(ref, ref, rt_s.at[i, d], rt_r.at[i, d], y_peer(d)).wait_recv()

    rows_wait()
    with scope("ranks_0"):
        for k in (9, 10, 7, 8):
            first(k)
    ag_step(10)
    with scope("ranks_1"):
        for k in (5, 6, 3):
            first(k)
    ag_step(11)
    with scope("ranks_2"):
        first(11)
        first(12)
        x_send(1)
        first(4)
    ag_step(12)
    with scope("ranks_3"):
        for k in range(3):
            first(k)
        x_send(0)
        x_reduce(1)
    ag_step(13)
    with scope("ranks_4"):
        first(13)
        first(14)
        whole_send(0, 0, 2)
        x_finish(1)
        sums(12)
        sums(11)
    ag_step(14)
    with scope("far_rows_out"):
        far_rows_send()
    with scope("ranks_5"):
        first(15)
        whole_send(1, 2, 3)
    with scope("whole_0"):
        whole_finish(0, 0, 2)
        far_ranks_send(0)
    with scope("whole_1"):
        whole_finish(1, 2, 3)
        far_ranks_send(1)
    with scope("reduce_0"):
        x_reduce(0)
        sums(10)
        sums(9)
    with scope("far_sums"):
        far_sums()

    def piece(v, c):
        s, h = SUM_HOPS - c // 2, c % 2
        return (above(s) if v == 0 else below(s)), pl.ds(half * (h if v == 0 else 1 - h), half)

    def rs_step(c):
        with scope(f"sum_hop_{c}"):
            for v, dev in enumerate((up, down)):
                k, part_rows = piece(v, c)
                x = part[k, part_rows, :]
                if c >= 2:
                    ref = prec.at[v, c - 2]
                    remote(ref, ref, rs_s.at[v, c - 2], rs_r.at[v, c - 2], dev).wait_recv()
                    x = x + prec[v, c - 2].astype(F32)
                psend[v, c] = x.astype(BF16)
                go(psend.at[v, c], prec.at[v, c], rs_s.at[v, c], rs_r.at[v, c], dev)

    rs_step(0)
    rs_step(1)
    with scope("base_out"):
        for d in range(1, NM):
            p = lax.rem(m + d, NM)
            go(fs.at[p], fr.at[m], f_s.at[d], f_r.at[d], m_peer(d))
    for i, s in enumerate(range(SUM_HOPS - 1, 0, -1)):
        with scope("sums"):
            if i:
                sums(2 * s)
                sums(2 * s - 1)
        rs_step(2 + 2 * i)
        if i == 0:
            with scope("rows_back_b"):
                x_finish(0)
                for k in range(5):
                    rows_back(k)
        if i == 1:
            with scope("rows_back_c"):
                for k in range(5, 8):
                    rows_back(k)
                ret_send(0, 0, 8)
        if i == 2:
            with scope("rows_back_d"):
                for k in range(10, 13):
                    rows_back(k)
        if i == 4:
            with scope("base_wait"):
                acc = fs[m]
                for d in range(1, NM):
                    src = lax.rem(m + NM - d, NM)
                    remote(fr.at[src], fr.at[src], f_s.at[d], f_r.at[d], m_peer(d)).wait_recv()
                    acc = acc + fr[src]
                fs[m] = acc
        rs_step(3 + 2 * i)
        if i in (0, 1):
            with scope("rows_back_e"):
                rows_back(8 + i)
        if i == 2:
            with scope("rows_back_f"):
                for k in range(13, 16):
                    rows_back(k)
                ret_send(1, 8, 16)
    sums(0)
    with scope("returned_wait"):
        ret_wait(0, 0, 8)
        ret_wait(1, 8, 16)
    with scope("outputs"):
        mine = ret[...].reshape(NY * NZ * PAD, wide)
        for j in range(4):
            r = pl.ds(128 * j, 128)
            place = back_place[r]
            ua[r] = (fg[r] + dot(place, mine[:, :feats], 1, 0)).astype(BF16)
            proj[r] = (fs[m, r] + dot(place, mine[:, feats:], 1, 0)).astype(BF16)
        tig_out = pltpu.make_async_copy(ua, tig_ref, loc.at[5])
        proj_out = pltpu.make_async_copy(proj, proj_ref, loc.at[6])
        tig_out.start()
        proj_out.start()
    with scope("last_sums"):
        for v, dev in enumerate((up, down)):
            for c in (SUMS - 2, SUMS - 1):
                ref = prec.at[v, c]
                remote(ref, ref, rs_s.at[v, c], rs_r.at[v, c], dev).wait_recv()
        for p in range(2):
            scale = SCALE * (1 - flags_ref[p]).astype(F32)
            c0, c1 = (SUMS - 2, SUMS - 1) if p == 0 else (SUMS - 1, SUMS - 2)
            r = slice(p * half, (p + 1) * half)
            v = scale * (part[0, r] + prec[0, c0].astype(F32) + prec[1, c1].astype(F32))
            down_ref[r] = v[:, :feats].astype(BF16)
            upg_ref[r] = v[:, feats:].astype(BF16)
    with scope("sent"):
        tig_out.wait()
        proj_out.wait()
        for c in started:
            c.wait_send()


def fused(tokens, weight, at, b, ids, panel_of, flags, upstream):
    rows, feats = tokens.shape
    n = at.shape[0]
    half = n // 2
    wide = feats + 128
    vm = pl.BlockSpec(memory_space=pltpu.VMEM)
    hbm = pl.BlockSpec(memory_space=pl.ANY)
    dma = pltpu.SemaphoreType.DMA
    group = NY * PAD
    nb = len(BATCHES)
    return pl.pallas_call(
        kernel,
        out_shape=(
            jax.ShapeDtypeStruct((rows, 128), BF16),
            jax.ShapeDtypeStruct((rows, feats), BF16),
            jax.ShapeDtypeStruct((n, feats), BF16),
            jax.ShapeDtypeStruct((n, 128), BF16),
        ),
        in_specs=[hbm, hbm, hbm, hbm, hbm, hbm, pl.BlockSpec(memory_space=pltpu.SMEM), hbm],
        out_specs=(hbm, hbm, vm, vm),
        scratch_shapes=[
            pltpu.VMEM((rows, feats), BF16),
            pltpu.VMEM(weight.shape, BF16),
            pltpu.VMEM(ids.shape, jnp.int32),
            pltpu.VMEM(panel_of.shape, jnp.int32),
            pltpu.VMEM(upstream.shape, BF16),
            pltpu.VMEM((rows, NM * 128), BF16),
            pltpu.VMEM((NM, rows, 128), F32),
            pltpu.VMEM((NM, rows, 128), F32),
            pltpu.VMEM((rows, feats), F32),
            pltpu.VMEM((rows, NY * NZ * PAD), BF16),
            pltpu.VMEM((NY, NZ, PAD, wide), BF16),
            pltpu.VMEM((NY, NZ, PAD, wide), BF16),
            pltpu.VMEM((NZ, n, wide), BF16),
            pltpu.VMEM((NZ, group, wide), BF16),
            pltpu.VMEM((NY, NZ, PAD, wide), BF16),
            pltpu.VMEM((NZ, group, 128), F32),
            pltpu.VMEM((NM, NZ, group // NM, 128), F32),
            pltpu.VMEM((NZ, group, 128), F32),
            pltpu.VMEM((3, group, 128), BF16),
            pltpu.VMEM((NM, 3, group, 128), BF16),
            pltpu.VMEM((2, group + group // 2, wide), BF16),
            pltpu.VMEM((2, group + group // 2, 128), F32),
            pltpu.VMEM((rows, 128), BF16),
            pltpu.VMEM((NZ, n, wide), F32),
            pltpu.VMEM((2, SUMS, half, wide), BF16),
            pltpu.VMEM((2, SUMS, half, wide), BF16),
            dma((2, CHUNKS)), dma((2, CHUNKS)),
            dma((NY,)), dma((NY,)),
            dma((2, NY)), dma((2, NY)),
            dma((nb, NM)), dma((nb, NM)),
            dma((nb, NM)), dma((nb, NM)),
            dma((2, SUMS)), dma((2, SUMS)),
            dma((NM,)), dma((NM,)),
            dma((NM,)), dma((NM,)),
            dma((2, NM)), dma((2, NM)),
            dma((4,)), dma((4,)),
            dma((4,)), dma((4,)),
            dma((12,)),
        ],
        compiler_params=pltpu.CompilerParams(
            collective_id=0, has_side_effects=True, vmem_limit_bytes=58 * 2**20
        ),
        cost_estimate=pl.CostEstimate(flops=5 * 10**9, bytes_accessed=10**7, transcendentals=0),
    )(tokens, weight, at, b, ids, panel_of, flags, upstream)


def copies(*refs):
    n = (len(refs) - 2) // 3
    ins, outs, bufs, (in_sems, out_sems) = refs[:n], refs[n : 2 * n], refs[2 * n : 3 * n], refs[3 * n :]
    parts = []
    for i in range(n):
        cuts = 4 if ins[i].shape[0] * ins[i].shape[1] > 2**18 else 1
        step = ins[i].shape[0] // cuts
        for j in range(cuts):
            r = pl.ds(step * j, step)
            k = len(parts)
            parts.append((
                pltpu.make_async_copy(ins[i].at[r], bufs[i].at[r], in_sems.at[k]),
                pltpu.make_async_copy(bufs[i].at[r], outs[i].at[r], out_sems.at[k]),
            ))
    for c, _ in parts:
        c.start()
    for c, d in parts:
        c.wait()
        d.start()
    for _, d in parts:
        d.wait()


def settle(arrays):
    hbm = pl.BlockSpec(memory_space=pl.ANY)
    dma = pltpu.SemaphoreType.DMA
    return pl.pallas_call(
        copies,
        out_shape=tuple(jax.ShapeDtypeStruct(a.shape, a.dtype) for a in arrays),
        in_specs=[hbm] * len(arrays),
        out_specs=(hbm,) * len(arrays),
        scratch_shapes=[pltpu.VMEM(a.shape, a.dtype) for a in arrays]
        + [dma((4 * len(arrays),)), dma((4 * len(arrays),))],
    )(*arrays)


def shards(tokens, base_weight, adapter_a, adapter_b, row_ids, panel_of, stop_flags, upstream):
    per_owner, feats, rank = adapter_a.shape
    vals = upstream.shape[1]
    at = jnp.transpose(adapter_a, (0, 2, 1)).reshape(per_owner * rank, feats)
    b = adapter_b.reshape(per_owner * rank, vals)
    projected, gradient, down, up = settle(fused(
        tokens, base_weight, at, b, row_ids.reshape(1, -1), panel_of.reshape(1, -1), stop_flags, upstream
    ))
    return (
        projected,
        gradient,
        jnp.transpose(down.reshape(per_owner, rank, feats), (0, 2, 1)),
        up.reshape(per_owner, rank, vals),
    )


def solution(mesh):
    fine = Mesh(mesh.devices.reshape(NY, NZ, NX, NC), ("y", "z", "x", "core"))
    placed = (
        P(DP, MP),
        P(MP, None),
        P(DP, MP, None),
        P(DP, None, MP),
        P(DP),
        P(),
        P(DP),
        P(DP, MP),
    )
    return jax.shard_map(
        shards,
        mesh=fine,
        in_specs=placed,
        out_specs=(P(DP, MP), P(DP, MP), P(DP, MP, None), P(DP, None, MP)),
        check_vma=False,
    )
```
